512 devices in a mesh: section: 2 (over z_hi), ctx: 32 (over x, y, core), head: 8 (over z_lo).
Axes of the slice: x: 4, y: 4, z: 16 (z_hi: 2, z_lo: 8; z = z_hi * 8 + z_lo), core: 2. Of those that a mesh axis runs over, the one named last changes fastest.
Arguments:
- residual_incoming: bfloat16 [3072, 16384], P('ctx', 'head'), may hold values from -44 to 44
- norm_gain: float32 [2, 16384], P('section'), may hold values from 0.1 to 1.9
- key_states: bfloat16 [2, 3072, 8, 128], P('section', ('ctx', 'head')), may hold values from -30 to 30
- value_states: bfloat16 [2, 3072, 8, 128], P('section', ('ctx', 'head')), may hold values from -5 to 5
- positions: int32 [3072], P(('ctx', 'head')), may hold values from 0 to 3071, as said below
Outputs:
- layer_outputs: bfloat16 [2, 3072, 16384], P('section', 'ctx', 'head')
The draws below stay inside these ranges and needn't reach their ends.
Inputs may be any that keep to these rules, and one draw needn't show every extreme that they name: positions is a permutation of 0 to 3071. Split the positions into runs of 48; the 96 stored rows of each index of ctx hold, in order, two whole runs i and (number of runs - 1 - i), with i differing between indices.
All inputs are finite; a program needn't handle non-finite values.
Results may differ from the reference program's by a relative error of at most 0.0075.
Values may be sent and summed in bfloat16 or wider, within the bound.
A program may use at most 64 MiB of HBM per device.

```python
import math
import jax
import jax.numpy as jnp
from jax import lax

D = 16384
HEADS = 128
KV_HEADS = 8
HEAD_DIM = 128
LAYERS = 2
SEQ = 3072
SPAN = 48
N_SECTION = 2
N_CTX = 32


def paired_positions(key):
    pair_order = jax.random.permutation(jax.random.fold_in(key, 101), N_CTX)
    row_index = jnp.arange(SEQ, dtype=jnp.int32)
    rank_of = row_index // (2 * SPAN)
    within = row_index % (2 * SPAN)
    upper_half = within // SPAN
    offset = within % SPAN
    pair_index = pair_order[rank_of]
    block_id = jnp.where(upper_half == 0, pair_index, 2 * N_CTX - 1 - pair_index)
    return (block_id * SPAN + offset).astype(jnp.int32)


def draw_positions(key, part):
    return paired_positions(key)


def draw_residual_incoming(key, part):
    key = jax.random.fold_in(key, 2)
    key_base, key_rows, key_cols = jax.random.split(key, 3)
    row_scale = jnp.exp(jax.random.uniform(key_rows, (SEQ, 1), jnp.float32, math.log(0.3), math.log(3.0)))
    col_place = jnp.arange(D, dtype=jnp.float32)[None, :] / D
    col_scale = jnp.exp(math.log(3.0) * col_place + jax.random.uniform(key_cols, (1, D), jnp.float32, math.log(0.4), math.log(1.2)))
    base_field = jnp.clip(jax.random.normal(key_base, (SEQ, D), jnp.float32), -4.0, 4.0)
    field_out = base_field * row_scale * col_scale
    return field_out.astype(jnp.bfloat16)


def draw_key_states(key, part):
    key = jax.random.fold_in(key, 3)
    full_shape = (N_SECTION, SEQ, KV_HEADS, HEAD_DIM)
    base_field = jnp.clip(jax.random.normal(key, full_shape, jnp.float32), -4.0, 4.0)
    return base_field.astype(jnp.bfloat16)


def level_of(stream_key, dims, cuts, least, top_value):
    gain = 1.0
    for dim, shards_of in cuts:
        steps = jax.random.uniform(jax.random.fold_in(jax.random.fold_in(stream_key, 6), dim), (shards_of,), jnp.float32, least / len(cuts), top_value / len(cuts))
        gain = gain * jnp.repeat(jnp.exp(steps), dims[dim] // shards_of).reshape((-1,) + (1,) * (len(dims) - 1 - dim))
    return gain


def normal_values(key, extent, scale, most, cuts=(), kind=jnp.bfloat16):
    entries = jax.random.normal(key, extent, jnp.float32) * scale
    if len(cuts) > 0:
        entries = level_of(key, extent, cuts, -0.22, 0.18) * entries
    return jnp.clip(entries, min=-most, max=most).astype(kind)


def setup_inputs(seed: int = 0) -> dict:
    splits = jax.random.split(jax.random.key(seed), 6)
    residual_incoming = draw_residual_incoming(jax.random.fold_in(splits[5], 71), 0)
    norm_gain = jnp.clip(1.0 + 0.18 * jax.random.normal(splits[1], (LAYERS, D), jnp.float32), 0.1, 1.9)
    key_states = draw_key_states(jax.random.fold_in(splits[5], 71), 0)
    value_states = normal_values(splits[3], (LAYERS, SEQ, KV_HEADS, HEAD_DIM), 1.0, 5.0, ((0, 2), (1, 256)))
    positions = draw_positions(jax.random.fold_in(splits[5], 71), 0)
    return {"residual_incoming": residual_incoming, "norm_gain": norm_gain, "key_states": key_states, "value_states": value_states, "positions": positions}


epsilon = 1e-05

def attend(queries, key_rows, value_matrix_rows, positions):
    group_size = HEADS // KV_HEADS
    query_heads = jnp.swapaxes(queries, 0, 1)
    key_heads = jnp.swapaxes(key_rows, 0, 1)
    value_heads = jnp.swapaxes(value_matrix_rows, 0, 1)
    visible = positions[:, None] >= positions[None, :]
    score_scale = 1.0 / math.sqrt(HEAD_DIM)

    def head_result(head_index):
        kv_index = head_index // group_size
        scores = jnp.dot(query_heads[head_index], key_heads[kv_index].T, preferred_element_type=jnp.float32) * score_scale
        scores = jnp.where(visible, scores, jnp.float32(-1e+30))
        row_max = lax.optimization_barrier(jnp.max(scores, axis=1, keepdims=True))
        weights = jnp.where(visible, jnp.exp(scores - row_max), jnp.float32(0.0))
        totals = lax.optimization_barrier(jnp.sum(weights, axis=1, keepdims=True))
        mixed_rows = jnp.dot(weights.astype(jnp.bfloat16), value_heads[kv_index], preferred_element_type=jnp.float32)
        return (mixed_rows / totals).astype(jnp.bfloat16)
    result = lax.map(head_result, jnp.arange(HEADS, dtype=jnp.int32))
    return jnp.swapaxes(result, 0, 1)

def apply_layer(inputs, gain_row, key_rows, value_matrix_rows, positions):
    widened = inputs.astype(jnp.float32)
    mean_square = lax.optimization_barrier(jnp.mean(widened * widened, axis=1, keepdims=True))
    normed = widened * lax.rsqrt(mean_square + epsilon) * gain_row[None, :]
    queries = normed.astype(jnp.bfloat16).reshape(SEQ, HEADS, HEAD_DIM)
    attended = attend(queries, key_rows, value_matrix_rows, positions).reshape(SEQ, D)
    return (widened + attended.astype(jnp.float32)).astype(jnp.bfloat16)

def reference(residual_incoming, norm_gain, key_states, value_states, positions):
    first_out = apply_layer(residual_incoming, norm_gain[0], key_states[0], value_states[0], positions)
    second = apply_layer(first_out, norm_gain[1], key_states[1], value_states[1], positions)
    return jnp.stack([first_out, second])
```

```python
import math

import jax
import jax.numpy as jnp
from jax import lax
from jax.sharding import PartitionSpec as P

HEAD_DIM = 128


epsilon = 1e-05


def update(state_now, query_tile_rows, key_tile_rows, value_block, query_pos, key_pos, score_scale):
    running_max, running_total_sum, weighted = state_now
    scores = (
        jnp.einsum(
            "ijvr,tjr->jvit", query_tile_rows, key_tile_rows, preferred_element_type=jnp.float32
        )
        * score_scale
    )
    visible = query_pos[:, None] >= key_pos[None, :]
    scores = jnp.where(visible, scores, jnp.float32(-1e30))
    new_max = jnp.maximum(running_max, jnp.max(scores, axis=-1))
    weights = jnp.where(visible, jnp.exp(scores - new_max[..., None]), jnp.float32(0.0))
    factor = jnp.exp(running_max - new_max)
    running_total_sum = running_total_sum * factor + jnp.sum(weights, axis=-1)
    weighted = weighted * factor[..., None] + jnp.einsum(
        "rlwo,orm->rlwm",
        weights.astype(jnp.bfloat16),
        value_block,
        preferred_element_type=jnp.float32,
    )
    return (new_max, running_total_sum, weighted)


def attend(queries, keys_piece, values_piece, every_pos, rank_pos):
    worker_rows, heads_dev, head_size = queries.shape
    half_rows = worker_rows // 2
    grouped = queries.reshape(2, half_rows, 1, heads_dev, head_size)
    query_pos = rank_pos.reshape(2, half_rows)
    score_scale = 1.0 / math.sqrt(head_size)
    start_state = (
        jnp.full((2, 1, heads_dev, half_rows), -1e30, jnp.float32),
        jnp.zeros((2, 1, heads_dev, half_rows), jnp.float32),
        jnp.zeros((2, 1, heads_dev, half_rows, head_size), jnp.float32),
    )
    block_rows = 512
    block_count = keys_piece.shape[0] // block_rows

    def key_block_step(block_index, state_now):
        start = block_index * block_rows
        key_tile_rows = lax.dynamic_slice_in_dim(keys_piece, start, block_rows, 0)
        value_block = lax.dynamic_slice_in_dim(values_piece, start, block_rows, 0)
        key_pos = lax.dynamic_slice_in_dim(every_pos, start, block_rows, 0)
        results = [
            update(
                tuple(part[half] for part in state_now),
                grouped[half],
                key_tile_rows,
                value_block,
                query_pos[half],
                key_pos,
                score_scale,
            )
            for half in range(2)
        ]
        return tuple(jnp.stack([results[0][k], results[1][k]]) for k in range(3))

    running_max, running_total_sum, weighted = lax.fori_loop(
        0, block_count, key_block_step, start_state
    )
    result = (weighted / running_total_sum[..., None]).astype(jnp.bfloat16)
    return result.transpose(0, 3, 1, 2, 4).reshape(worker_rows, heads_dev, head_size)


SPAN = 48


def local(residual_incoming, norm_gain, key_states, value_states, positions):
    section = lax.axis_index("section")
    head = lax.axis_index("head")
    heads = lax.axis_size("head")
    rows, cols = residual_incoming.shape
    width = cols * heads
    runs = 2 * lax.axis_size("ctx")
    run = positions[0] // SPAN
    first_run = jnp.where(head * positions.shape[0] < SPAN, run, runs - 1 - run)
    mine = jnp.concatenate([key_states, value_states], axis=0).astype(jnp.bfloat16)
    other = lax.ppermute(mine, "section", [(0, 1)])
    other_gain = lax.ppermute(norm_gain, "section", [(0, 1)])
    is_first = section == 0
    lower = jnp.where(is_first, mine, other)
    lower_gain = jnp.where(is_first, norm_gain, other_gain)

    def gather(pair):
        swapped = lax.all_to_all(pair, "head", split_axis=2, concat_axis=1, tiled=True)
        block = swapped.reshape(2 * rows, HEAD_DIM)
        meta = jnp.full((16, HEAD_DIM), first_run.astype(jnp.bfloat16), jnp.bfloat16)
        block = jnp.concatenate([block, meta], axis=0)
        whole = lax.all_gather(block, "ctx", axis=0)
        first = whole[:, 2 * rows, 0].astype(jnp.int32)
        both = jnp.stack([first, runs - 1 - first], axis=1).reshape(-1)
        pos = (both[:, None] * SPAN + jnp.arange(SPAN, dtype=jnp.int32)[None, :]).reshape(-1)
        keys = whole[:, :rows].reshape(-1, 1, HEAD_DIM)
        values = whole[:, rows : 2 * rows].reshape(-1, 1, HEAD_DIM)
        return keys, values, pos

    own = jnp.stack([first_run, runs - 1 - first_run])
    rank_pos = (own[:, None] * SPAN + jnp.arange(SPAN, dtype=jnp.int32)[None, :]).reshape(-1)

    def apply_layer(inputs, gain, gathered):
        wide = inputs.astype(jnp.float32)
        squares = lax.psum(jnp.sum(wide * wide, axis=1), "head")
        gain_part = lax.dynamic_slice_in_dim(gain[0], head * cols, cols, 0)
        scale = lax.rsqrt(squares / width + epsilon)[:, None]
        normed = (wide * scale * gain_part[None, :]).astype(jnp.bfloat16)
        mixed = attend(normed.reshape(rows, -1, HEAD_DIM), *gathered, rank_pos)
        return (wide + mixed.reshape(rows, cols).astype(jnp.float32)).astype(jnp.bfloat16)

    first_out = apply_layer(residual_incoming, lower_gain, gather(lower))
    second = apply_layer(first_out, norm_gain, gather(mine))
    return jnp.where(is_first, first_out, second)[None]


def solution(mesh):
    placed = (
        P("ctx", "head"),
        P("section", None),
        P("section", ("ctx", "head"), None, None),
        P("section", ("ctx", "head"), None, None),
        P(("ctx", "head")),
    )
    return jax.shard_map(
        local, mesh=mesh, in_specs=placed, out_specs=P("section", "ctx", "head"), check_vma=False
    )
```

```python
import functools
import math

import jax
import jax.numpy as jnp
from jax import lax
from jax.experimental import pallas as pl
from jax.experimental.pallas import tpu as pltpu
from jax.sharding import PartitionSpec as P

HEAD_DIM = 128
SPAN = 48
EPSILON = 1e-05
ROWS = 2 * SPAN
SLOT = 2 * ROWS + 16
CHIPS = 16
SIDE = 4
HEADS_AXIS = 8
SECTIONS = 2
CTX = 2 * CHIPS
RUNS = 2 * CTX
PIECE = ROWS // HEADS_AXIS
KEY_BLOCK = 256
ROW_TILE = 192
GROUP = 16
Q_ROWS = GROUP * SPAN
SCALE = math.log2(math.e) / math.sqrt(HEAD_DIM)
F32 = jnp.float32
BF16 = jnp.bfloat16


def iota(shape, dim):
    return lax.broadcasted_iota(jnp.int32, shape, dim)


def first_run_of(pos_ref, head):
    run = pos_ref[0] // SPAN
    return jnp.where(head * PIECE < SPAN, run, RUNS - 1 - run)


def square_rows(wide_tiles):
    total = wide_tiles[0] * wide_tiles[0]
    for tile in wide_tiles[1:]:
        total = total + tile * tile
    padded = jnp.concatenate([total, jnp.zeros((HEAD_DIM - ROWS, HEAD_DIM), F32)], axis=0)
    turned = padded.T
    part = turned[0:8]
    for k in range(1, HEAD_DIM // 8):
        part = part + turned[8 * k : 8 * k + 8]
    return part


def exchange_kernel(
    k_ref,
    v_ref,
    pos_ref,
    x_ref,
    gain_ref,
    g0_ref,
    g1_ref,
    gain0_ref,
    sq_ref,
    zsend,
    zrecv0,
    zrecv1,
    stage,
    sq_own,
    gain_own,
    zs_sem,
    zr0_sem,
    zr1_sem,
    sqs_sem,
    sqr_sem,
    gain_sem,
    gs_sem,
    gr_sem,
    fs_sem,
    fr_sem,
    own_sem,
):
    section = lax.axis_index("section")
    ctx = lax.axis_index("ctx")
    head = lax.axis_index("head")
    chip = ctx // 2
    core = ctx % 2
    cx = chip // SIDE
    cy = chip % SIDE
    sibling = ctx + 1 - 2 * core

    def at(offset, sign):
        dx, dy = offset // SIDE, offset % SIDE
        px = lax.rem(cx + sign * dx + SIDE, SIDE)
        py = lax.rem(cy + sign * dy + SIDE, SIDE)
        return (px * SIDE + py) * 2 + core

    def head_at(offset, sign):
        return lax.rem(head + sign * offset + HEADS_AXIS, HEADS_AXIS)

    def remote(src, dst, send, recv, s=None, c=None, h=None):
        target = (
            section if s is None else s,
            ctx if c is None else c,
            head if h is None else h,
        )
        return pltpu.make_async_remote_copy(
            src_ref=src,
            dst_ref=dst,
            send_sem=send,
            recv_sem=recv,
            device_id=target,
            device_id_type=pl.DeviceIdType.MESH,
        )

    barrier = pltpu.get_barrier_semaphore()

    def greet(s, c, h):
        pl.semaphore_signal(
            barrier, inc=1, device_id=(s, c, h), device_id_type=pl.DeviceIdType.MESH
        )

    for d in range(1, HEADS_AXIS):
        greet(section, ctx, head_at(d, 1))
    for d in range(HEADS_AXIS):
        greet(1 - section, ctx, head_at(d, 1))
    for d in range(1, CHIPS):
        greet(section, at(d, 1), head)
    greet(section, sibling, head)

    out_row = iota((HEAD_DIM, ROWS), 0)
    in_row = iota((HEAD_DIM, ROWS), 1)
    pick = (out_row % 16) * HEADS_AXIS + out_row // 16
    spread = jnp.where((in_row == pick) & (out_row % 16 < PIECE), 1.0, 0.0).astype(BF16)
    keys = jnp.dot(spread, k_ref[...], preferred_element_type=F32).astype(BF16)
    values = jnp.dot(spread, v_ref[...], preferred_element_type=F32).astype(BF16)
    for h in range(HEADS_AXIS):
        zsend[h, 0:16] = keys[16 * h : 16 * h + 16]
        zsend[h, 16:32] = values[16 * h : 16 * h + 16]
    gain_own[...] = gain_ref[pl.ds(pl.multiple_of(head * GROUP, GROUP), GROUP), :]
    wide = [
        x_ref[:, HEAD_DIM * a : HEAD_DIM * (a + 1)].astype(F32) for a in range(GROUP)
    ]
    sq_own[...] = square_rows(wide)
    first_run = first_run_of(pos_ref, head)
    swap = first_run >= CTX
    low = jnp.where(swap, RUNS - 1 - first_run, first_run)

    pl.semaphore_wait(barrier, 2 * HEADS_AXIS - 1 + CHIPS)

    sq_copies = [
        remote(sq_own, sq_ref.at[head], sqs_sem.at[d], sqr_sem.at[d], h=head_at(d, 1))
        for d in range(1, HEADS_AXIS)
    ]

    @pl.when(section == 0)
    def _():
        for d in range(HEADS_AXIS):
            peer = head_at(d, 1)
            remote(
                zsend.at[peer],
                zrecv0.at[head],
                zs_sem.at[d],
                zr0_sem.at[d],
                s=1,
                h=peer,
            ).start()
            if d > 0:
                remote(
                    zsend.at[peer],
                    zrecv0.at[head],
                    zs_sem.at[HEADS_AXIS + d],
                    zr0_sem.at[d],
                    h=peer,
                ).start()
        zrecv0[head] = zsend[head]
        remote(gain_own, gain0_ref, gain_sem.at[0], gain_sem.at[1], s=1).start()

    @pl.when(section == 1)
    def _():
        for d in range(1, HEADS_AXIS):
            peer = head_at(d, 1)
            remote(
                zsend.at[peer],
                zrecv1.at[head],
                zs_sem.at[d],
                zr1_sem.at[d],
                h=peer,
            ).start()
        zrecv1[head] = zsend[head]

    for copy in sq_copies:
        copy.start()
    own_sq = pltpu.make_async_copy(sq_own, sq_ref.at[head], own_sem.at[2])
    own_sq.start()

    row = iota((2 * ROWS, 16 * 16), 0)
    col = iota((2 * ROWS, 16 * 16), 1)
    turn = jnp.where(swap, SPAN, 0)
    place = lax.rem(row + turn, ROWS)
    source = (place // PIECE) * 32 + place % PIECE + jnp.where(row >= ROWS, 16, 0)
    compact = jnp.where(col == source, 1.0, 0.0).astype(BF16)
    meta = jnp.zeros((16, HEAD_DIM), F32) + low.astype(F32)

    def begin_layer(layer, zrecv, g_ref):
        pieces = zrecv[...].reshape(16 * 16, HEAD_DIM)
        block = jnp.dot(compact, pieces, preferred_element_type=F32).astype(BF16)
        stage[layer, 0 : 2 * ROWS] = block
        stage[layer, 2 * ROWS : SLOT] = meta.astype(BF16)
        for d in range(1, CHIPS):
            remote(
                stage.at[layer],
                g_ref.at[ctx],
                gs_sem.at[layer, d],
                gr_sem.at[layer, d],
                c=at(d, 1),
            ).start()
        remote(
            stage.at[layer],
            g_ref.at[ctx],
            fs_sem.at[layer, 0],
            fr_sem.at[layer, 0],
            c=sibling,
        ).start()
        pltpu.make_async_copy(stage.at[layer], g_ref.at[ctx], own_sem.at[layer]).start()

    def relay(layer, g_ref, d):
        got = at(d, -1)
        remote(
            stage.at[layer],
            g_ref.at[got],
            gs_sem.at[layer, d],
            gr_sem.at[layer, d],
            c=at(d, 1),
        ).wait_recv()
        remote(
            g_ref.at[got],
            g_ref.at[got],
            fs_sem.at[layer, d],
            fr_sem.at[layer, d],
            c=sibling,
        ).start()

    def end_layer(layer, g_ref):
        for d in range(CHIPS):
            got = at(d, -1)
            slot = got + 1 - 2 * core
            if d > 0:
                remote(
                    stage.at[layer],
                    g_ref.at[ctx],
                    gs_sem.at[layer, d],
                    gr_sem.at[layer, d],
                    c=at(d, 1),
                ).wait_send()
            mine = stage.at[layer] if d == 0 else g_ref.at[got]
            remote(
                mine,
                g_ref.at[got],
                fs_sem.at[layer, d],
                fr_sem.at[layer, d],
                c=sibling,
            ).wait_send()
            remote(
                mine,
                g_ref.at[slot],
                fs_sem.at[layer, d],
                fr_sem.at[layer, d],
                c=sibling,
            ).wait_recv()
        pltpu.make_async_copy(stage.at[layer], g_ref.at[ctx], own_sem.at[layer]).wait()

    @pl.when(section == 1)
    def _():
        remote(
            zsend.at[head], zrecv0.at[head], zs_sem.at[0], zr0_sem.at[0], s=0
        ).wait_recv()

    for d in range(1, HEADS_AXIS):
        got = head_at(d, -1)
        remote(
            zsend.at[got], zrecv0.at[got], zs_sem.at[d], zr0_sem.at[d], h=got
        ).wait_recv()
    begin_layer(0, zrecv0, g0_ref)

    @pl.when(section == 1)
    def _():
        for d in range(1, HEADS_AXIS):
            got = head_at(d, -1)
            remote(
                zsend.at[got], zrecv1.at[got], zs_sem.at[d], zr1_sem.at[d], h=got
            ).wait_recv()
        begin_layer(1, zrecv1, g1_ref)

    for d in range(1, CHIPS):
        relay(0, g0_ref, d)

    @pl.when(section == 1)
    def _():
        for d in range(1, CHIPS):
            relay(1, g1_ref, d)

    end_layer(0, g0_ref)

    @pl.when(section == 1)
    def _():
        end_layer(1, g1_ref)
        for d in range(1, HEADS_AXIS):
            peer = head_at(d, 1)
            remote(
                zsend.at[peer], zrecv1.at[head], zs_sem.at[d], zr1_sem.at[d], h=peer
            ).wait_send()
        remote(gain_own, gain0_ref, gain_sem.at[0], gain_sem.at[1], s=0).wait_recv()

    @pl.when(section == 0)
    def _():
        for d in range(HEADS_AXIS):
            peer = head_at(d, 1)
            remote(
                zsend.at[peer], zrecv0.at[head], zs_sem.at[d], zr0_sem.at[d], s=1, h=peer
            ).wait_send()
            if d > 0:
                remote(
                    zsend.at[peer],
                    zrecv0.at[head],
                    zs_sem.at[HEADS_AXIS + d],
                    zr0_sem.at[d],
                    h=peer,
                ).wait_send()
        remote(gain_own, gain0_ref, gain_sem.at[0], gain_sem.at[1], s=1).wait_send()
        keep = pltpu.make_async_copy(gain_own, gain0_ref, own_sem.at[3])
        keep.start()
        keep.wait()

    for d in range(1, HEADS_AXIS):
        got = head_at(d, -1)
        sq_copies[d - 1].wait_send()
        remote(sq_own, sq_ref.at[got], sqs_sem.at[d], sqr_sem.at[d], h=got).wait_recv()
    own_sq.wait()


def exchange(keys, values, positions, x, gain):
    any_space = pl.BlockSpec(memory_space=pl.ANY)
    vmem = pl.BlockSpec(memory_space=pltpu.VMEM)
    smem = pl.BlockSpec(memory_space=pltpu.SMEM)
    dma = pltpu.SemaphoreType.DMA
    return pl.pallas_call(
        exchange_kernel,
        name="exchange_keys",
        out_shape=(
            jax.ShapeDtypeStruct((CTX, SLOT, HEAD_DIM), BF16),
            jax.ShapeDtypeStruct((CTX, SLOT, HEAD_DIM), BF16),
            jax.ShapeDtypeStruct((GROUP, HEAD_DIM), F32),
            jax.ShapeDtypeStruct((HEADS_AXIS, 8, HEAD_DIM), F32),
        ),
        in_specs=[vmem, vmem, smem, vmem, vmem],
        out_specs=(any_space, any_space, any_space, any_space),
        scratch_shapes=[
            pltpu.VMEM((HEADS_AXIS, 32, HEAD_DIM), BF16),
            pltpu.VMEM((HEADS_AXIS, 32, HEAD_DIM), BF16),
            pltpu.VMEM((HEADS_AXIS, 32, HEAD_DIM), BF16),
            pltpu.VMEM((2, SLOT, HEAD_DIM), BF16),
            pltpu.VMEM((8, HEAD_DIM), F32),
            pltpu.VMEM((GROUP, HEAD_DIM), F32),
            dma((2 * HEADS_AXIS,)),
            dma((HEADS_AXIS,)),
            dma((HEADS_AXIS,)),
            dma((HEADS_AXIS,)),
            dma((HEADS_AXIS,)),
            dma((2,)),
            dma((2, CHIPS)),
            dma((2, CHIPS)),
            dma((2, CHIPS)),
            dma((2, CHIPS)),
            dma((4,)),
        ],
        compiler_params=pltpu.CompilerParams(collective_id=0, has_side_effects=True),
    )(keys, values, positions, x, gain)


def sums_kernel(part_ref, out_ref, send_sem, recv_sem):
    section = lax.axis_index("section")
    ctx = lax.axis_index("ctx")
    head = lax.axis_index("head")
    barrier = pltpu.get_barrier_semaphore()

    def peer(d, sign):
        return (section, ctx, lax.rem(head + sign * d + HEADS_AXIS, HEADS_AXIS))

    def copy(d, slot, device):
        return pltpu.make_async_remote_copy(
            src_ref=part_ref,
            dst_ref=out_ref.at[slot],
            send_sem=send_sem.at[d],
            recv_sem=recv_sem.at[d],
            device_id=device,
            device_id_type=pl.DeviceIdType.MESH,
        )

    for d in range(1, HEADS_AXIS):
        pl.semaphore_signal(
            barrier, inc=1, device_id=peer(d, 1), device_id_type=pl.DeviceIdType.MESH
        )
    pl.semaphore_wait(barrier, HEADS_AXIS - 1)
    for d in range(1, HEADS_AXIS):
        copy(d, head, peer(d, 1)).start()
    out_ref[head] = part_ref[...]
    for d in range(1, HEADS_AXIS):
        copy(d, head, peer(d, 1)).wait_send()
        copy(d, peer(d, -1)[2], peer(d, -1)).wait_recv()


def exchange_sums(part):
    vmem = pl.BlockSpec(memory_space=pltpu.VMEM)
    return pl.pallas_call(
        sums_kernel,
        name="exchange_sums",
        out_shape=jax.ShapeDtypeStruct((HEADS_AXIS, 8, HEAD_DIM), F32),
        in_specs=[vmem],
        out_specs=vmem,
        scratch_shapes=[
            pltpu.SemaphoreType.DMA((HEADS_AXIS,)),
            pltpu.SemaphoreType.DMA((HEADS_AXIS,)),
        ],
        compiler_params=pltpu.CompilerParams(collective_id=1, has_side_effects=True),
    )(part)


def attend_rows(q_ref, ks, vs, m_ref, l_ref, acc_ref, half, run):
    clear = SPAN * run // KEY_BLOCK
    blocks = (SPAN * (run + 1) + KEY_BLOCK - 1) // KEY_BLOCK
    m_ref[...] = jnp.full(m_ref.shape, -1e30, F32)
    l_ref[...] = jnp.zeros(l_ref.shape, F32)
    acc_ref[...] = jnp.zeros(acc_ref.shape, F32)

    def step(block, masked):
        start = pl.multiple_of(block * KEY_BLOCK, KEY_BLOCK)
        k = ks[pl.ds(start, KEY_BLOCK), :]
        v = vs[pl.ds(start, KEY_BLOCK), :]
        for t in range(Q_ROWS // ROW_TILE):
            here = pl.ds(t * ROW_TILE, ROW_TILE)
            q = q_ref[half, t * ROW_TILE : (t + 1) * ROW_TILE, :]
            s = lax.dot_general(
                q, k, (((1,), (1,)), ((), ())), preferred_element_type=F32
            )
            if masked:
                key_pos = start + iota(s.shape, 1)
                query_pos = run * SPAN + iota(s.shape, 0) % SPAN
                s = jnp.where(key_pos <= query_pos, s, -1e30)
            old = m_ref[here, :]
            new = jnp.maximum(old, jnp.max(s, axis=1, keepdims=True))
            wide = jnp.concatenate([new] * (KEY_BLOCK // HEAD_DIM), axis=1)
            p = jnp.exp2((s - wide) * SCALE)
            factor = jnp.exp2((old - new) * SCALE)
            lanes = p[:, :HEAD_DIM]
            for k2 in range(1, KEY_BLOCK // HEAD_DIM):
                lanes = lanes + p[:, HEAD_DIM * k2 : HEAD_DIM * (k2 + 1)]
            l_ref[here, :] = l_ref[here, :] * factor + lanes
            acc_ref[here, :] = acc_ref[here, :] * factor + jnp.dot(
                p.astype(BF16), v, preferred_element_type=F32
            )
            m_ref[here, :] = new

    lax.fori_loop(0, clear, lambda block, carry: step(block, False), None)
    lax.fori_loop(clear, blocks, lambda block, carry: step(block, True), None)


def attention_kernel(
    last,
    x_ref,
    g_ref,
    sq_ref,
    gain_ref,
    pos_ref,
    y_ref,
    part_ref,
    ks,
    vs,
    q_ref,
    m_ref,
    l_ref,
    acc_ref,
    table,
    table_s,
    sem,
):
    head = lax.axis_index("head")
    section = lax.axis_index("section")

    def work():
        tags = jnp.max(g_ref[:, 2 * ROWS : SLOT, :].astype(F32), axis=1)
        slot_id = iota((CTX, HEAD_DIM), 0)
        lane = iota((CTX, HEAD_DIM), 1)
        order = jnp.sum(
            jnp.where(tags == lane.astype(F32), slot_id, 0).astype(F32), axis=0, keepdims=True
        )
        table[...] = jnp.broadcast_to(order.astype(jnp.int32), (8, HEAD_DIM))
        fetch = pltpu.make_async_copy(table, table_s, sem)
        fetch.start()

        total = sq_ref[0]
        for d in range(1, HEADS_AXIS):
            total = total + sq_ref[d]
        total = jnp.sum(total, axis=0, keepdims=True)
        scale = lax.rsqrt(total * (1.0 / (HEADS_AXIS * GROUP * HEAD_DIM)) + EPSILON)
        column = jnp.broadcast_to(scale, (HEAD_DIM, HEAD_DIM)).T[:ROWS]
        for a in range(GROUP):
            wide = x_ref[:, HEAD_DIM * a : HEAD_DIM * (a + 1)].astype(F32)
            q = (wide * column * gain_ref[a : a + 1, :]).astype(BF16)
            q_ref[0, SPAN * a : SPAN * (a + 1), :] = q[:SPAN]
            q_ref[1, SPAN * a : SPAN * (a + 1), :] = q[SPAN:]
        fetch.wait()
        for t in range(CTX):
            c = table_s[0, t]
            lo = slice(SPAN * t, SPAN * (t + 1))
            hi = slice(SPAN * (RUNS - 1 - t), SPAN * (RUNS - t))
            ks[lo, :] = g_ref[c, 0:SPAN, :]
            ks[hi, :] = g_ref[c, SPAN:ROWS, :]
            vs[lo, :] = g_ref[c, ROWS : ROWS + SPAN, :]
            vs[hi, :] = g_ref[c, ROWS + SPAN : 2 * ROWS, :]
        first_run = first_run_of(pos_ref, head)
        for half in range(2):
            run = first_run if half == 0 else RUNS - 1 - first_run
            attend_rows(q_ref, ks, vs, m_ref, l_ref, acc_ref, half, run)
            for a in range(GROUP):
                here = slice(SPAN * a, SPAN * (a + 1))
                total_w = jnp.sum(l_ref[here, :], axis=1, keepdims=True)
                mixed = (acc_ref[here, :] / total_w).astype(BF16).astype(F32)
                rows = slice(SPAN * half, SPAN * (half + 1))
                cols = slice(HEAD_DIM * a, HEAD_DIM * (a + 1))
                y_ref[rows, cols] = (x_ref[rows, cols].astype(F32) + mixed).astype(BF16)

    if last:

        @pl.when(section == 1)
        def _():
            work()

        @pl.when(section == 0)
        def _():
            y_ref[...] = x_ref[...]

    else:
        work()
        part_ref[...] = square_rows(
            [y_ref[:, HEAD_DIM * a : HEAD_DIM * (a + 1)].astype(F32) for a in range(GROUP)]
        )


def attention(last, x, gathered, sums, gain, positions):
    vmem = pl.BlockSpec(memory_space=pltpu.VMEM)
    smem = pl.BlockSpec(memory_space=pltpu.SMEM)
    kernel = functools.partial(attention_kernel, last)
    out_shape = [jax.ShapeDtypeStruct(x.shape, BF16)]
    if last:
        inner = kernel

        def kernel(*refs):
            inner(*refs[:6], None, *refs[6:])
    else:
        out_shape.append(jax.ShapeDtypeStruct((8, HEAD_DIM), F32))
    keys = RUNS * SPAN
    return pl.pallas_call(
        kernel,
        name="attend_last" if last else "attend_first",
        out_shape=tuple(out_shape),
        in_specs=[vmem, vmem, vmem, vmem, smem],
        out_specs=tuple([vmem] * len(out_shape)),
        scratch_shapes=[
            pltpu.VMEM((keys, HEAD_DIM), BF16),
            pltpu.VMEM((keys, HEAD_DIM), BF16),
            pltpu.VMEM((2, Q_ROWS, HEAD_DIM), BF16),
            pltpu.VMEM((Q_ROWS, HEAD_DIM), F32),
            pltpu.VMEM((Q_ROWS, HEAD_DIM), F32),
            pltpu.VMEM((Q_ROWS, HEAD_DIM), F32),
            pltpu.VMEM((8, HEAD_DIM), jnp.int32),
            pltpu.SMEM((8, HEAD_DIM), jnp.int32),
            pltpu.SemaphoreType.DMA,
        ],
        compiler_params=pltpu.CompilerParams(vmem_limit_bytes=48 * 2**20),
    )(x, gathered, sums, gain, positions)


def local(residual_incoming, norm_gain, key_states, value_states, positions):
    head = lax.axis_index("head")
    x = residual_incoming
    keys = key_states.reshape(ROWS, HEAD_DIM)
    values = value_states.reshape(ROWS, HEAD_DIM)
    gain = norm_gain.reshape(-1, HEAD_DIM)
    g0, g1, gain0, sums0 = exchange(keys, values, positions, x, gain)
    own_gain = lax.dynamic_slice_in_dim(gain, head * GROUP, GROUP, 0)
    first_out, part = attention(False, x, g0, sums0, gain0, positions)
    sums1 = exchange_sums(part)
    (out,) = attention(True, first_out, g1, sums1, own_gain, positions)
    return out[None]


def solution(mesh):
    placed = (
        P("ctx", "head"),
        P("section", None),
        P("section", ("ctx", "head"), None, None),
        P("section", ("ctx", "head"), None, None),
        P(("ctx", "head")),
    )
    return jax.shard_map(
        local, mesh=mesh, in_specs=placed, out_specs=P("section", "ctx", "head"), check_vma=False
    )
```

```python
import math

import jax
import jax.numpy as jnp
from jax import lax
from jax.experimental import pallas as pl
from jax.experimental.pallas import tpu as pltpu
from jax.sharding import PartitionSpec as P

HEAD_DIM = 128
SPAN = 48
EPSILON = 1e-05
ROWS = 2 * SPAN
SLOT = 2 * ROWS + 16
CHIPS = 16
SIDE = 4
HEADS_AXIS = 8
SECTIONS = 2
CTX = 2 * CHIPS
RUNS = 2 * CTX
PIECE = ROWS // HEADS_AXIS
WAVE = 2 * SIDE
TOKENS = 16
TILE = 16 * TOKENS
TILES = SPAN // TOKENS
GROUP = 16
SCALE = math.log2(math.e) / math.sqrt(HEAD_DIM)
SECOND_AFTER = 1
ORDER = tuple(SIDE * dx + dy for dx in range(SIDE) for dy in (1, 3, 2, 0) if dx + dy > 0)
F32 = jnp.float32
BF16 = jnp.bfloat16


def iota(shape, dim):
    return lax.broadcasted_iota(jnp.int32, shape, dim)


def first_run_of(pos_ref, head):
    run = pos_ref[0] // SPAN
    return jnp.where(head * PIECE < SPAN, run, RUNS - 1 - run)


def square_rows(wide_tiles):
    total = wide_tiles[0] * wide_tiles[0]
    for tile in wide_tiles[1:]:
        total = total + tile * tile
    padded = jnp.concatenate([total, jnp.zeros((HEAD_DIM - ROWS, HEAD_DIM), F32)], axis=0)
    turned = padded.T
    part = turned[0:8]
    for k in range(1, HEAD_DIM // 8):
        part = part + turned[8 * k : 8 * k + 8]
    return part


def column_scale(parts):
    total = parts[0]
    for d in range(1, HEADS_AXIS):
        total = total + parts[d]
    total = jnp.sum(total, axis=0, keepdims=True)
    scale = lax.rsqrt(total * (1.0 / (HEADS_AXIS * GROUP * HEAD_DIM)) + EPSILON)
    return jnp.broadcast_to(scale, (HEAD_DIM, HEAD_DIM)).T


def update(q, k, v, old, gap):
    s = lax.dot_general(q, k, (((1,), (1,)), ((), ())), preferred_element_type=F32)
    s = jnp.where(gap <= iota(s.shape, 0) % TOKENS, s, -1e30)
    new = jnp.maximum(old[0], jnp.max(s, axis=1, keepdims=True))
    parts = s.shape[1] // HEAD_DIM
    p = jnp.exp2((s - jnp.concatenate([new] * parts, axis=1)) * SCALE)
    total = p[:, :HEAD_DIM]
    for i in range(1, parts):
        total = total + p[:, HEAD_DIM * i : HEAD_DIM * (i + 1)]
    mixed = jnp.dot(p.astype(BF16), v, preferred_element_type=F32)
    factor = jnp.exp2((old[0] - new) * SCALE)
    return new, old[1] * factor + total, old[2] * factor + mixed


def sublayers_kernel(
    k_ref,
    v_ref,
    pos_ref,
    x_hbm,
    gain_ref,
    out_ref,
    x_ref,
    k_own,
    v_own,
    zsend,
    zrecv0,
    zrecv1,
    stage,
    g0_ref,
    g1_ref,
    gain0,
    gain_own,
    sq_own,
    sq0,
    sq1,
    y_ref,
    q_ref,
    m_ref,
    l_ref,
    acc_ref,
    zs_sem,
    zr0_sem,
    zr1_sem,
    sqs_sem,
    sqr_sem,
    gain_sem,
    gs_sem,
    gr_sem,
    fs_sem,
    fr_sem,
    in_sem,
):
    section = lax.axis_index("section")
    ctx = lax.axis_index("ctx")
    head = lax.axis_index("head")
    chip = ctx // 2
    core = ctx % 2
    cx = chip // SIDE
    cy = chip % SIDE
    sibling = ctx + 1 - 2 * core

    def at(offset, sign):
        dx, dy = offset // SIDE, offset % SIDE
        px = lax.rem(cx + sign * dx + SIDE, SIDE)
        py = lax.rem(cy + sign * dy + SIDE, SIDE)
        return (px * SIDE + py) * 2 + core

    def head_at(offset, sign):
        return lax.rem(head + sign * offset + HEADS_AXIS, HEADS_AXIS)

    def remote(src, dst, send, recv, s=None, c=None, h=None):
        target = (
            section if s is None else s,
            ctx if c is None else c,
            head if h is None else h,
        )
        return pltpu.make_async_remote_copy(
            src_ref=src,
            dst_ref=dst,
            send_sem=send,
            recv_sem=recv,
            device_id=target,
            device_id_type=pl.DeviceIdType.MESH,
        )

    own_rows = pl.ds(pl.multiple_of(head * GROUP, GROUP), GROUP)
    fetches = [
        pltpu.make_async_copy(src, dst, in_sem.at[i])
        for i, (src, dst) in enumerate(
            (
                (k_ref, k_own),
                (v_ref, v_own),
                (x_hbm, x_ref),
                (gain_ref.at[own_rows], gain_own),
            )
        )
    ]
    for fetch in fetches:
        fetch.start()

    barrier = pltpu.get_barrier_semaphore()

    def greet(s, c, h):
        pl.semaphore_signal(
            barrier, inc=1, device_id=(s, c, h), device_id_type=pl.DeviceIdType.MESH
        )

    @pl.when(section == 1)
    def _():
        for d in range(HEADS_AXIS):
            greet(0, ctx, head_at(d, 1))

    for d in range(1, HEADS_AXIS):
        greet(section, ctx, head_at(d, 1))
    for d in range(1, CHIPS):
        greet(section, at(d, 1), head)
    greet(section, sibling, head)

    out_row = iota((HEAD_DIM, ROWS), 0)
    in_row = iota((HEAD_DIM, ROWS), 1)
    pick = (out_row % 16) * HEADS_AXIS + out_row // 16
    spread = jnp.where((in_row == pick) & (out_row % 16 < PIECE), 1.0, 0.0).astype(BF16)
    fetches[0].wait()
    fetches[1].wait()
    keys = jnp.dot(spread, k_own[...], preferred_element_type=F32).astype(BF16)
    values = jnp.dot(spread, v_own[...], preferred_element_type=F32).astype(BF16)
    for h in range(HEADS_AXIS):
        zsend[h, 0:16] = keys[16 * h : 16 * h + 16]
        zsend[h, 16:32] = values[16 * h : 16 * h + 16]
    fetches[2].wait()
    fetches[3].wait()
    sq_own[0] = square_rows(
        [x_ref[:, HEAD_DIM * a : HEAD_DIM * (a + 1)].astype(F32) for a in range(GROUP)]
    )
    sq0[head] = sq_own[0]
    first_run = first_run_of(pos_ref, head)
    swap = first_run >= CTX
    low = jnp.where(swap, RUNS - 1 - first_run, first_run)

    @pl.when(section == 0)
    def _():
        pl.semaphore_wait(barrier, 2 * HEADS_AXIS - 1 + CHIPS)
        for d in range(HEADS_AXIS):
            peer = head_at(d, 1)
            remote(
                zsend.at[peer],
                zrecv0.at[head],
                zs_sem.at[d],
                zr0_sem.at[d],
                s=1,
                h=peer,
            ).start()
            if d > 0:
                remote(
                    zsend.at[peer],
                    zrecv0.at[head],
                    zs_sem.at[HEADS_AXIS + d],
                    zr0_sem.at[d],
                    h=peer,
                ).start()
        zrecv0[head] = zsend[head]
        gain0[...] = gain_own[...]
        remote(gain_own, gain0, gain_sem.at[0], gain_sem.at[1], s=1).start()

    @pl.when(section == 1)
    def _():
        pl.semaphore_wait(barrier, HEADS_AXIS - 1 + CHIPS)
        for d in range(1, HEADS_AXIS):
            peer = head_at(d, 1)
            remote(
                zsend.at[peer],
                zrecv1.at[head],
                zs_sem.at[d],
                zr1_sem.at[d],
                h=peer,
            ).start()
        zrecv1[head] = zsend[head]

    def send_sums(part, sq):
        for d in range(1, HEADS_AXIS):
            remote(
                sq_own.at[part],
                sq.at[head],
                sqs_sem.at[part, d],
                sqr_sem.at[part, d],
                h=head_at(d, 1),
            ).start()

    def finish_sums(part, sq):
        for d in range(1, HEADS_AXIS):
            remote(
                sq_own.at[part],
                sq.at[head_at(d, -1)],
                sqs_sem.at[part, d],
                sqr_sem.at[part, d],
                h=head_at(d, 1),
            ).wait()

    send_sums(0, sq0)

    row = iota((2 * ROWS, 16 * 16), 0)
    col = iota((2 * ROWS, 16 * 16), 1)
    turn = jnp.where(swap, SPAN, 0)
    place = lax.rem(row + turn, ROWS)
    source = (place // PIECE) * 32 + place % PIECE + jnp.where(row >= ROWS, 16, 0)
    compact = jnp.where(col == source, 1.0, 0.0).astype(BF16)
    meta = (jnp.zeros((16, HEAD_DIM), F32) + low.astype(F32)).astype(BF16)

    def begin_layer(layer, zrecv, g_ref):
        pieces = zrecv[...].reshape(16 * 16, HEAD_DIM)
        block = jnp.dot(compact, pieces, preferred_element_type=F32).astype(BF16)
        stage[layer, 0 : 2 * ROWS] = block
        stage[layer, 2 * ROWS : SLOT] = meta
        remote(
            stage.at[layer],
            g_ref.at[ctx],
            fs_sem.at[layer, 0],
            fr_sem.at[layer, 0],
            c=sibling,
        ).start()
        for d in ORDER:
            remote(
                stage.at[layer],
                g_ref.at[ctx],
                gs_sem.at[layer, d],
                gr_sem.at[layer, d],
                c=at(d, 1),
            ).start()
        g_ref[ctx, 0 : 2 * ROWS] = block
        g_ref[ctx, 2 * ROWS : SLOT] = meta

    def relay(layer, g_ref, d):
        got = at(d, -1)
        remote(
            stage.at[layer],
            g_ref.at[got],
            gs_sem.at[layer, d],
            gr_sem.at[layer, d],
            c=at(d, 1),
        ).wait_recv()
        remote(
            g_ref.at[got],
            g_ref.at[got],
            fs_sem.at[layer, d],
            fr_sem.at[layer, d],
            c=sibling,
        ).start()

    def relayed(layer, g_ref, d, own=False):
        slot = at(d, -1) + 1 - 2 * core
        mine = stage.at[layer] if own else g_ref.at[at(d, -1)]
        remote(
            mine, g_ref.at[slot], fs_sem.at[layer, d], fr_sem.at[layer, d], c=sibling
        ).wait_recv()

    def sent(layer, g_ref):
        for d in range(CHIPS):
            if d > 0:
                remote(
                    stage.at[layer],
                    g_ref.at[ctx],
                    gs_sem.at[layer, d],
                    gr_sem.at[layer, d],
                    c=at(d, 1),
                ).wait_send()
            mine = stage.at[layer] if d == 0 else g_ref.at[at(d, -1)]
            remote(
                mine, g_ref.at[ctx], fs_sem.at[layer, d], fr_sem.at[layer, d], c=sibling
            ).wait_send()

    @pl.when(section == 1)
    def _():
        remote(
            zsend.at[head], zrecv0.at[head], zs_sem.at[0], zr0_sem.at[0], s=0
        ).wait_recv()

    for d in range(1, HEADS_AXIS):
        got = head_at(d, -1)
        remote(
            zsend.at[got], zrecv0.at[got], zs_sem.at[d], zr0_sem.at[d], h=got
        ).wait_recv()
    begin_layer(0, zrecv0, g0_ref)

    def clear_state():
        m_ref[...] = jnp.full(m_ref.shape, -1e30, F32)
        l_ref[...] = jnp.zeros(l_ref.shape, F32)
        acc_ref[...] = jnp.zeros(acc_ref.shape, F32)

    clear_state()

    def make_queries(h_ref, sq, gain, tiles):
        column = column_scale([sq[d] for d in range(HEADS_AXIS)])
        for tile in tiles:
            for a in range(GROUP):
                cols = slice(HEAD_DIM * a, HEAD_DIM * (a + 1))
                qs = []
                for half in range(2):
                    rows = slice(half * SPAN + tile * TOKENS, half * SPAN + (tile + 1) * TOKENS)
                    wide = h_ref[rows, cols].astype(F32)
                    qs.append(wide * column[rows] * gain[a : a + 1, :])
                to = slice(TOKENS * a, TOKENS * (a + 1))
                q_ref[0, tile, to, :] = jnp.where(swap, qs[1], qs[0]).astype(BF16)
                q_ref[1, tile, to, :] = jnp.where(swap, qs[0], qs[1]).astype(BF16)

    def load_state(slot, tile):
        return m_ref[slot, tile], l_ref[slot, tile], acc_ref[slot, tile]

    def store_state(slot, tile, state):
        m_ref[slot, tile], l_ref[slot, tile], acc_ref[slot, tile] = state

    def attend_wave(g_ref, dx, tiles):
        row_of = lax.rem(cx - dx + SIDE, SIDE)
        here = pl.ds(row_of * WAVE, WAVE)
        size = 2 * WAVE * SPAN
        lane = iota((1, size), 1)
        tag = jnp.zeros((1, size), F32)
        tags = g_ref[here, 2 * ROWS : SLOT, :].astype(F32)
        for i in range(WAVE):
            wide = jnp.concatenate([tags[i, 0:1, :]] * (size // HEAD_DIM), axis=1)
            tag = jnp.where(lane // ROWS == i, wide, tag)
        at_row = lane % ROWS
        run = tag.astype(jnp.int32)
        run = jnp.where(at_row >= SPAN, RUNS - 1 - run, run)
        key_pos = run * SPAN + at_row % SPAN
        low_lane = iota((1, size // 2), 1)
        tag = jnp.zeros((1, size // 2), F32)
        for i in range(WAVE):
            wide = jnp.concatenate([tags[i, 0:1, :]] * (size // 2 // HEAD_DIM), axis=1)
            tag = jnp.where(low_lane // SPAN == i, wide, tag)
        low_pos = tag.astype(jnp.int32) * SPAN + low_lane % SPAN
        k = g_ref[here, 0:ROWS, :].reshape(size, HEAD_DIM)
        v = g_ref[here, ROWS : 2 * ROWS, :].reshape(size, HEAD_DIM)
        k_low = g_ref[here, 0:SPAN, :].reshape(size // 2, HEAD_DIM)
        v_low = g_ref[here, ROWS : ROWS + SPAN, :].reshape(size // 2, HEAD_DIM)
        for tile in tiles:
            start = (RUNS - 1 - low) * SPAN + tile * TOKENS
            state = update(q_ref[1, tile], k, v, load_state(1, tile), key_pos - start)
            store_state(1, tile, state)
            start = low * SPAN + tile * TOKENS
            state = update(
                q_ref[0, tile], k_low, v_low, load_state(0, tile), low_pos - start
            )
            store_state(0, tile, state)

    def write_rows(h_ref, to_ref, tiles):
        for tile in tiles:
            mixed = []
            for kind in range(2):
                total = jnp.sum(l_ref[kind, tile], axis=1, keepdims=True)
                mixed.append(acc_ref[kind, tile] / total)
            halves = (
                jnp.where(swap, mixed[1], mixed[0]).astype(BF16).astype(F32),
                jnp.where(swap, mixed[0], mixed[1]).astype(BF16).astype(F32),
            )
            for half in range(2):
                r0 = half * SPAN + tile * TOKENS
                rows = slice(r0, r0 + TOKENS)
                for a in range(GROUP):
                    cols = slice(HEAD_DIM * a, HEAD_DIM * (a + 1))
                    part = halves[half][TOKENS * a : TOKENS * (a + 1)]
                    to_ref[rows, cols] = (h_ref[rows, cols].astype(F32) + part).astype(BF16)

    def receive_wave(layer, g_ref, dx):
        @pl.when(dx == 0)
        def _():
            relayed(layer, g_ref, 0, True)

        @pl.when(dx > 0)
        def _():
            relay(layer, g_ref, dx * SIDE)

        for dy in range(1, SIDE):
            relay(layer, g_ref, dx * SIDE + dy)

        @pl.when(dx > 0)
        def _():
            relayed(layer, g_ref, dx * SIDE)

        for dy in range(1, SIDE):
            relayed(layer, g_ref, dx * SIDE + dy)

    finish_sums(0, sq0)

    @pl.when(section == 1)
    def _():
        remote(gain_own, gain0, gain_sem.at[0], gain_sem.at[1], s=0).wait_recv()
        for d in range(1, HEADS_AXIS):
            got = head_at(d, -1)
            remote(
                zsend.at[got], zrecv1.at[got], zs_sem.at[d], zr1_sem.at[d], h=got
            ).wait_recv()

    every = range(TILES)
    make_queries(x_ref, sq0, gain0, every)

    def early(dx, carry):
        receive_wave(0, g0_ref, dx)

        @pl.when((section == 1) & (dx == SECOND_AFTER))
        def _():
            begin_layer(1, zrecv1, g1_ref)

        attend_wave(g0_ref, dx, every)
        return carry

    lax.fori_loop(0, SIDE - 1, early, 0)

    first, rest = range(0, 1), range(1, TILES)

    def squares_of(part, sq):
        sq_own[part] = square_rows(
            [y_ref[:, HEAD_DIM * a : HEAD_DIM * (a + 1)].astype(F32) for a in range(GROUP)]
        )
        sq[head] = sq_own[part]
        send_sums(part, sq)

    y_ref[...] = x_ref[...]
    receive_wave(0, g0_ref, jnp.int32(SIDE - 1))
    attend_wave(g0_ref, SIDE - 1, first)
    write_rows(x_ref, y_ref, first)

    @pl.when(section == 1)
    def _():
        squares_of(1, sq1.at[0])

    attend_wave(g0_ref, SIDE - 1, rest)
    write_rows(x_ref, y_ref, rest)

    @pl.when(section == 0)
    def _():
        out_ref[...] = y_ref[...]

    @pl.when(section == 1)
    def _():
        squares_of(2, sq1.at[1])
        clear_state()
        finish_sums(1, sq1.at[0])
        make_queries(y_ref, sq1.at[0], gain_own, first)

        def with_relay(dx, carry):
            receive_wave(1, g1_ref, dx)
            attend_wave(g1_ref, dx, first)
            return carry

        lax.fori_loop(0, SIDE, with_relay, 0)
        write_rows(y_ref, out_ref, first)
        finish_sums(2, sq1.at[1])
        make_queries(y_ref, sq1.at[1], gain_own, rest)

        def without_relay(dx, carry):
            attend_wave(g1_ref, dx, rest)
            return carry

        lax.fori_loop(0, SIDE, without_relay, 0)
        write_rows(y_ref, out_ref, rest)
        sent(1, g1_ref)
        for d in range(1, HEADS_AXIS):
            peer = head_at(d, 1)
            remote(
                zsend.at[peer], zrecv1.at[head], zs_sem.at[d], zr1_sem.at[d], h=peer
            ).wait_send()

    sent(0, g0_ref)

    @pl.when(section == 0)
    def _():
        for d in range(HEADS_AXIS):
            peer = head_at(d, 1)
            remote(
                zsend.at[peer], zrecv0.at[head], zs_sem.at[d], zr0_sem.at[d], s=1, h=peer
            ).wait_send()
            if d > 0:
                remote(
                    zsend.at[peer],
                    zrecv0.at[head],
                    zs_sem.at[HEADS_AXIS + d],
                    zr0_sem.at[d],
                    h=peer,
                ).wait_send()
        remote(gain_own, gain0, gain_sem.at[0], gain_sem.at[1], s=1).wait_send()


def local(residual_incoming, norm_gain, key_states, value_states, positions):
    vmem = pl.BlockSpec(memory_space=pltpu.VMEM)
    smem = pl.BlockSpec(memory_space=pltpu.SMEM)
    dma = pltpu.SemaphoreType.DMA
    state = pltpu.VMEM((2, TILES, TILE, HEAD_DIM), F32)
    pieces = pltpu.VMEM((HEADS_AXIS, 32, HEAD_DIM), BF16)
    blocks = pltpu.VMEM((CTX, SLOT, HEAD_DIM), BF16)
    anywhere = pl.BlockSpec(memory_space=pl.ANY)
    rows = pltpu.VMEM((ROWS, HEAD_DIM), BF16)
    out = pl.pallas_call(
        sublayers_kernel,
        name="sublayers",
        out_shape=jax.ShapeDtypeStruct(residual_incoming.shape, BF16),
        in_specs=[anywhere, anywhere, smem, anywhere, anywhere],
        out_specs=vmem,
        scratch_shapes=[
            pltpu.VMEM(residual_incoming.shape, BF16),
            rows,
            rows,
            pieces,
            pieces,
            pieces,
            pltpu.VMEM((2, SLOT, HEAD_DIM), BF16),
            blocks,
            blocks,
            pltpu.VMEM((GROUP, HEAD_DIM), F32),
            pltpu.VMEM((GROUP, HEAD_DIM), F32),
            pltpu.VMEM((3, 8, HEAD_DIM), F32),
            pltpu.VMEM((HEADS_AXIS, 8, HEAD_DIM), F32),
            pltpu.VMEM((2, HEADS_AXIS, 8, HEAD_DIM), F32),
            pltpu.VMEM(residual_incoming.shape, BF16),
            pltpu.VMEM((2, TILES, TILE, HEAD_DIM), BF16),
            state,
            state,
            state,
            dma((2 * HEADS_AXIS,)),
            dma((HEADS_AXIS,)),
            dma((HEADS_AXIS,)),
            dma((3, HEADS_AXIS)),
            dma((3, HEADS_AXIS)),
            dma((2,)),
            dma((2, CHIPS)),
            dma((2, CHIPS)),
            dma((2, CHIPS)),
            dma((2, CHIPS)),
            dma((4,)),
        ],
        compiler_params=pltpu.CompilerParams(
            collective_id=0, has_side_effects=True, vmem_limit_bytes=48 * 2**20
        ),
    )(
        key_states.reshape(ROWS, HEAD_DIM),
        value_states.reshape(ROWS, HEAD_DIM),
        positions,
        residual_incoming,
        norm_gain.reshape(-1, HEAD_DIM),
    )
    return out[None]


def solution(mesh):
    placed = (
        P("ctx", "head"),
        P("section", None),
        P("section", ("ctx", "head"), None, None),
        P("section", ("ctx", "head"), None, None),
        P(("ctx", "head")),
    )
    return jax.shard_map(
        local, mesh=mesh, in_specs=placed, out_specs=P("section", "ctx", "head"), check_vma=False
    )
```

```python
import math

import jax
import jax.numpy as jnp
from jax import lax
from jax.experimental import pallas as pl
from jax.experimental.pallas import tpu as pltpu
from jax.sharding import PartitionSpec as P

HEAD_DIM = 128
SPAN = 48
EPSILON = 1e-05
ROWS = 2 * SPAN
SLOT = 2 * ROWS + 16
CHIPS = 16
SIDE = 4
HEADS_AXIS = 8
SECTIONS = 2
CTX = 2 * CHIPS
RUNS = 2 * CTX
PIECE = ROWS // HEADS_AXIS
WAVE = 2 * SIDE
TOKENS = 16
TILE = 16 * TOKENS
TILES = SPAN // TOKENS
GROUP = 16
SCALE = math.log2(math.e) / math.sqrt(HEAD_DIM)
SECOND_AFTER = 2
ORDER = tuple(SIDE * dx + dy for dx in range(SIDE) for dy in (1, 3, 2, 0) if dx + dy > 0)
F32 = jnp.float32
BF16 = jnp.bfloat16


def iota(shape, dim):
    return lax.broadcasted_iota(jnp.int32, shape, dim)


def first_run_of(pos_ref, head):
    run = pos_ref[0] // SPAN
    return jnp.where(head * PIECE < SPAN, run, RUNS - 1 - run)


def square_rows(wide_tiles):
    total = wide_tiles[0] * wide_tiles[0]
    for tile in wide_tiles[1:]:
        total = total + tile * tile
    padded = jnp.concatenate([total, jnp.zeros((HEAD_DIM - ROWS, HEAD_DIM), F32)], axis=0)
    turned = padded.T
    part = turned[0:8]
    for k in range(1, HEAD_DIM // 8):
        part = part + turned[8 * k : 8 * k + 8]
    return part


def column_scale(parts):
    total = parts[0]
    for d in range(1, HEADS_AXIS):
        total = total + parts[d]
    total = jnp.sum(total, axis=0, keepdims=True)
    scale = lax.rsqrt(total * (1.0 / (HEADS_AXIS * GROUP * HEAD_DIM)) + EPSILON)
    return jnp.broadcast_to(scale, (HEAD_DIM, HEAD_DIM)).T


def update(q, k, v, old, gap, place):
    s = lax.dot_general(q, k, (((1,), (1,)), ((), ())), preferred_element_type=F32)
    parts = s.shape[1] // HEAD_DIM
    s = jnp.where(gap <= jnp.concatenate([place] * parts, axis=1), s, -1e30)
    new = jnp.maximum(old[0], jnp.max(s, axis=1, keepdims=True))
    p = jnp.exp2((s - jnp.concatenate([new] * parts, axis=1)) * SCALE)
    both = jnp.dot(p.astype(BF16), v, preferred_element_type=F32)
    factor = jnp.exp2((old[0] - new) * SCALE)
    return new, old[1] * factor + both[:, HEAD_DIM:], old[2] * factor + both[:, :HEAD_DIM]


def sublayers_kernel(
    k_ref,
    v_ref,
    pos_ref,
    x_hbm,
    gain_ref,
    out_ref,
    x_ref,
    k_own,
    v_own,
    zsend,
    zrecv0,
    zrecv1,
    stage,
    g0_ref,
    g1_ref,
    gain0,
    gain_own,
    sq_own,
    sq0,
    sq1,
    y_ref,
    q_ref,
    m_ref,
    l_ref,
    acc_ref,
    place_ref,
    zs_sem,
    zr0_sem,
    zr1_sem,
    sqs_sem,
    sqr_sem,
    gain_sem,
    gs_sem,
    gr_sem,
    fs_sem,
    fr_sem,
    in_sem,
):
    section = lax.axis_index("section")
    ctx = lax.axis_index("ctx")
    head = lax.axis_index("head")
    chip = ctx // 2
    core = ctx % 2
    cx = chip // SIDE
    cy = chip % SIDE
    sibling = ctx + 1 - 2 * core

    def at(offset, sign):
        dx, dy = offset // SIDE, offset % SIDE
        px = lax.rem(cx + sign * dx + SIDE, SIDE)
        py = lax.rem(cy + sign * dy + SIDE, SIDE)
        return (px * SIDE + py) * 2 + core

    def head_at(offset, sign):
        return lax.rem(head + sign * offset + HEADS_AXIS, HEADS_AXIS)

    def remote(src, dst, send, recv, s=None, c=None, h=None):
        target = (
            section if s is None else s,
            ctx if c is None else c,
            head if h is None else h,
        )
        return pltpu.make_async_remote_copy(
            src_ref=src,
            dst_ref=dst,
            send_sem=send,
            recv_sem=recv,
            device_id=target,
            device_id_type=pl.DeviceIdType.MESH,
        )

    own_rows = pl.ds(pl.multiple_of(head * GROUP, GROUP), GROUP)
    fetches = [
        pltpu.make_async_copy(src, dst, in_sem.at[i])
        for i, (src, dst) in enumerate(
            (
                (k_ref, k_own),
                (v_ref, v_own),
                (x_hbm, x_ref),
                (gain_ref.at[own_rows], gain_own),
            )
        )
    ]
    for fetch in fetches:
        fetch.start()

    barrier = pltpu.get_barrier_semaphore()

    def greet(s, c, h):
        pl.semaphore_signal(
            barrier, inc=1, device_id=(s, c, h), device_id_type=pl.DeviceIdType.MESH
        )

    @pl.when(section == 1)
    def _():
        for d in range(HEADS_AXIS):
            greet(0, ctx, head_at(d, 1))

    for d in range(1, HEADS_AXIS):
        greet(section, ctx, head_at(d, 1))
    for d in range(1, CHIPS):
        greet(section, at(d, 1), head)
    greet(section, sibling, head)

    out_row = iota((HEAD_DIM, ROWS), 0)
    in_row = iota((HEAD_DIM, ROWS), 1)
    pick = (out_row % 16) * HEADS_AXIS + out_row // 16
    spread = jnp.where((in_row == pick) & (out_row % 16 < PIECE), 1.0, 0.0).astype(BF16)
    fetches[0].wait()
    fetches[1].wait()
    keys = jnp.dot(spread, k_own[...], preferred_element_type=F32).astype(BF16)
    values = jnp.dot(spread, v_own[...], preferred_element_type=F32).astype(BF16)
    for h in range(HEADS_AXIS):
        zsend[h, 0:16] = keys[16 * h : 16 * h + 16]
        zsend[h, 16:32] = values[16 * h : 16 * h + 16]
    fetches[2].wait()
    fetches[3].wait()
    sq_own[0] = square_rows(
        [x_ref[:, HEAD_DIM * a : HEAD_DIM * (a + 1)].astype(F32) for a in range(GROUP)]
    )
    sq0[head] = sq_own[0]
    first_run = first_run_of(pos_ref, head)
    swap = first_run >= CTX
    low = jnp.where(swap, RUNS - 1 - first_run, first_run)

    @pl.when(section == 0)
    def _():
        pl.semaphore_wait(barrier, 2 * HEADS_AXIS - 1 + CHIPS)
        for d in range(HEADS_AXIS):
            peer = head_at(d, 1)
            remote(
                zsend.at[peer],
                zrecv0.at[head],
                zs_sem.at[d],
                zr0_sem.at[d],
                s=1,
                h=peer,
            ).start()
            if d > 0:
                remote(
                    zsend.at[peer],
                    zrecv0.at[head],
                    zs_sem.at[HEADS_AXIS + d],
                    zr0_sem.at[d],
                    h=peer,
                ).start()
        zrecv0[head] = zsend[head]
        gain0[...] = gain_own[...]
        remote(gain_own, gain0, gain_sem.at[0], gain_sem.at[1], s=1).start()

    @pl.when(section == 1)
    def _():
        pl.semaphore_wait(barrier, HEADS_AXIS - 1 + CHIPS)
        for d in range(1, HEADS_AXIS):
            peer = head_at(d, 1)
            remote(
                zsend.at[peer],
                zrecv1.at[head],
                zs_sem.at[d],
                zr1_sem.at[d],
                h=peer,
            ).start()
        zrecv1[head] = zsend[head]

    def send_sums(part, sq):
        for d in range(1, HEADS_AXIS):
            remote(
                sq_own.at[part],
                sq.at[head],
                sqs_sem.at[part, d],
                sqr_sem.at[part, d],
                h=head_at(d, 1),
            ).start()

    def finish_sums(part, sq):
        for d in range(1, HEADS_AXIS):
            remote(
                sq_own.at[part],
                sq.at[head_at(d, -1)],
                sqs_sem.at[part, d],
                sqr_sem.at[part, d],
                h=head_at(d, 1),
            ).wait()

    send_sums(0, sq0)

    row = iota((2 * ROWS, 16 * 16), 0)
    col = iota((2 * ROWS, 16 * 16), 1)
    turn = jnp.where(swap, SPAN, 0)
    place = lax.rem(row + turn, ROWS)
    source = (place // PIECE) * 32 + place % PIECE + jnp.where(row >= ROWS, 16, 0)
    compact = jnp.where(col == source, 1.0, 0.0).astype(BF16)
    meta = (jnp.zeros((16, HEAD_DIM), F32) + low.astype(F32)).astype(BF16)

    def begin_layer(layer, zrecv, g_ref):
        pieces = zrecv[...].reshape(16 * 16, HEAD_DIM)
        block = jnp.dot(compact, pieces, preferred_element_type=F32).astype(BF16)
        stage[layer, 0 : 2 * ROWS] = block
        stage[layer, 2 * ROWS : SLOT] = meta
        remote(
            stage.at[layer],
            g_ref.at[ctx],
            fs_sem.at[layer, 0],
            fr_sem.at[layer, 0],
            c=sibling,
        ).start()
        for d in ORDER:
            remote(
                stage.at[layer],
                g_ref.at[ctx],
                gs_sem.at[layer, d],
                gr_sem.at[layer, d],
                c=at(d, 1),
            ).start()
        g_ref[ctx, 0 : 2 * ROWS] = block
        g_ref[ctx, 2 * ROWS : SLOT] = meta

    def relay(layer, g_ref, d):
        got = at(d, -1)
        remote(
            stage.at[layer],
            g_ref.at[got],
            gs_sem.at[layer, d],
            gr_sem.at[layer, d],
            c=at(d, 1),
        ).wait_recv()
        remote(
            g_ref.at[got],
            g_ref.at[got],
            fs_sem.at[layer, d],
            fr_sem.at[layer, d],
            c=sibling,
        ).start()

    def relayed(layer, g_ref, d, own=False):
        slot = at(d, -1) + 1 - 2 * core
        mine = stage.at[layer] if own else g_ref.at[at(d, -1)]
        remote(
            mine, g_ref.at[slot], fs_sem.at[layer, d], fr_sem.at[layer, d], c=sibling
        ).wait_recv()

    def sent(layer, g_ref):
        for d in range(CHIPS):
            if d > 0:
                remote(
                    stage.at[layer],
                    g_ref.at[ctx],
                    gs_sem.at[layer, d],
                    gr_sem.at[layer, d],
                    c=at(d, 1),
                ).wait_send()
            mine = stage.at[layer] if d == 0 else g_ref.at[at(d, -1)]
            remote(
                mine, g_ref.at[ctx], fs_sem.at[layer, d], fr_sem.at[layer, d], c=sibling
            ).wait_send()

    @pl.when(section == 1)
    def _():
        remote(
            zsend.at[head], zrecv0.at[head], zs_sem.at[0], zr0_sem.at[0], s=0
        ).wait_recv()

    for d in range(1, HEADS_AXIS):
        got = head_at(d, -1)
        remote(
            zsend.at[got], zrecv0.at[got], zs_sem.at[d], zr0_sem.at[d], h=got
        ).wait_recv()
    begin_layer(0, zrecv0, g0_ref)

    def clear_state():
        m_ref[...] = jnp.full(m_ref.shape, -1e30, F32)
        l_ref[...] = jnp.zeros(l_ref.shape, F32)
        acc_ref[...] = jnp.zeros(acc_ref.shape, F32)

    clear_state()
    place_shape = (TILES, TILE, HEAD_DIM)
    place_ref[...] = iota(place_shape, 0) * TOKENS + iota(place_shape, 1) % TOKENS

    def make_queries(h_ref, sq, gain, tiles):
        column = column_scale([sq[d] for d in range(HEADS_AXIS)])
        for tile in tiles:
            for a in range(GROUP):
                cols = slice(HEAD_DIM * a, HEAD_DIM * (a + 1))
                qs = []
                for half in range(2):
                    rows = slice(half * SPAN + tile * TOKENS, half * SPAN + (tile + 1) * TOKENS)
                    wide = h_ref[rows, cols].astype(F32)
                    qs.append(wide * column[rows] * gain[a : a + 1, :])
                to = slice(TOKENS * a, TOKENS * (a + 1))
                q_ref[0, tile, to, :] = jnp.where(swap, qs[1], qs[0]).astype(BF16)
                q_ref[1, tile, to, :] = jnp.where(swap, qs[0], qs[1]).astype(BF16)

    def flat(ref, kind, tiles):
        rows = ref[kind, tiles.start : tiles.stop]
        return rows.reshape(len(tiles) * TILE, HEAD_DIM)

    def update_rows(kind, tiles, k, v, gap):
        old = tuple(flat(ref, kind, tiles) for ref in (m_ref, l_ref, acc_ref))
        place = place_ref[tiles.start : tiles.stop].reshape(len(tiles) * TILE, HEAD_DIM)
        state = update(flat(q_ref, kind, tiles), k, v, old, gap, place)
        for ref, part in zip((m_ref, l_ref, acc_ref), state):
            ref[kind, tiles.start : tiles.stop] = part.reshape(len(tiles), TILE, HEAD_DIM)

    def attend_wave(g_ref, dx, tiles):
        row_of = lax.rem(cx - dx + SIDE, SIDE)
        here = pl.ds(row_of * WAVE, WAVE)
        size = 2 * WAVE * SPAN
        lane = iota((1, size), 1)
        tag = jnp.zeros((1, size), F32)
        tags = g_ref[here, 2 * ROWS : SLOT, :].astype(F32)
        for i in range(WAVE):
            wide = jnp.concatenate([tags[i, 0:1, :]] * (size // HEAD_DIM), axis=1)
            tag = jnp.where(lane // ROWS == i, wide, tag)
        at_row = lane % ROWS
        run = tag.astype(jnp.int32)
        run = jnp.where(at_row >= SPAN, RUNS - 1 - run, run)
        key_pos = run * SPAN + at_row % SPAN
        low_lane = iota((1, size // 2), 1)
        tag = jnp.zeros((1, size // 2), F32)
        for i in range(WAVE):
            wide = jnp.concatenate([tags[i, 0:1, :]] * (size // 2 // HEAD_DIM), axis=1)
            tag = jnp.where(low_lane // SPAN == i, wide, tag)
        low_pos = tag.astype(jnp.int32) * SPAN + low_lane % SPAN
        k = g_ref[here, 0:ROWS, :].reshape(size, HEAD_DIM)
        v = g_ref[here, ROWS : 2 * ROWS, :].reshape(size, HEAD_DIM)
        k_low = g_ref[here, 0:SPAN, :].reshape(size // 2, HEAD_DIM)
        v_low = g_ref[here, ROWS : ROWS + SPAN, :].reshape(size // 2, HEAD_DIM)
        ones = jnp.ones((size, HEAD_DIM), BF16)
        v = jnp.concatenate([v, ones], axis=1)
        v_low = jnp.concatenate([v_low, ones[: size // 2]], axis=1)
        update_rows(1, tiles, k, v, key_pos - (RUNS - 1 - low) * SPAN)
        update_rows(0, tiles, k_low, v_low, low_pos - low * SPAN)

    def write_rows(h_ref, to_ref, tiles):
        for tile in tiles:
            mixed = []
            for kind in range(2):
                mixed.append(acc_ref[kind, tile] / l_ref[kind, tile])
            halves = (
                jnp.where(swap, mixed[1], mixed[0]).astype(BF16).astype(F32),
                jnp.where(swap, mixed[0], mixed[1]).astype(BF16).astype(F32),
            )
            for half in range(2):
                r0 = half * SPAN + tile * TOKENS
                rows = slice(r0, r0 + TOKENS)
                for a in range(GROUP):
                    cols = slice(HEAD_DIM * a, HEAD_DIM * (a + 1))
                    part = halves[half][TOKENS * a : TOKENS * (a + 1)]
                    to_ref[rows, cols] = (h_ref[rows, cols].astype(F32) + part).astype(BF16)

    def receive_wave(layer, g_ref, dx):
        @pl.when(dx == 0)
        def _():
            relayed(layer, g_ref, 0, True)

        @pl.when(dx > 0)
        def _():
            relay(layer, g_ref, dx * SIDE)

        for dy in range(1, SIDE):
            relay(layer, g_ref, dx * SIDE + dy)

        @pl.when(dx > 0)
        def _():
            relayed(layer, g_ref, dx * SIDE)

        for dy in range(1, SIDE):
            relayed(layer, g_ref, dx * SIDE + dy)

    finish_sums(0, sq0)

    @pl.when(section == 1)
    def _():
        remote(gain_own, gain0, gain_sem.at[0], gain_sem.at[1], s=0).wait_recv()
        for d in range(1, HEADS_AXIS):
            got = head_at(d, -1)
            remote(
                zsend.at[got], zrecv1.at[got], zs_sem.at[d], zr1_sem.at[d], h=got
            ).wait_recv()

    every = range(TILES)
    make_queries(x_ref, sq0, gain0, every)

    def early(dx, carry):
        receive_wave(0, g0_ref, dx)

        @pl.when((section == 1) & (dx == SECOND_AFTER))
        def _():
            begin_layer(1, zrecv1, g1_ref)

        attend_wave(g0_ref, dx, every)
        return carry

    lax.fori_loop(0, SIDE - 1, early, 0)

    first, rest = range(0, 1), range(1, TILES)

    def squares_of(part, sq):
        sq_own[part] = square_rows(
            [y_ref[:, HEAD_DIM * a : HEAD_DIM * (a + 1)].astype(F32) for a in range(GROUP)]
        )
        sq[head] = sq_own[part]
        send_sums(part, sq)

    y_ref[...] = x_ref[...]
    receive_wave(0, g0_ref, jnp.int32(SIDE - 1))
    attend_wave(g0_ref, SIDE - 1, first)
    write_rows(x_ref, y_ref, first)

    @pl.when(section == 1)
    def _():
        squares_of(1, sq1.at[0])

    attend_wave(g0_ref, SIDE - 1, rest)
    write_rows(x_ref, y_ref, rest)

    @pl.when(section == 0)
    def _():
        out_ref[...] = y_ref[...]

    @pl.when(section == 1)
    def _():
        squares_of(2, sq1.at[1])
        clear_state()
        finish_sums(1, sq1.at[0])
        make_queries(y_ref, sq1.at[0], gain_own, first)

        def with_relay(dx, carry):
            receive_wave(1, g1_ref, dx)
            attend_wave(g1_ref, dx, first)
            return carry

        lax.fori_loop(0, SIDE, with_relay, 0)
        write_rows(y_ref, out_ref, first)
        finish_sums(2, sq1.at[1])
        make_queries(y_ref, sq1.at[1], gain_own, rest)

        def without_relay(dx, carry):
            attend_wave(g1_ref, dx, rest)
            return carry

        lax.fori_loop(0, SIDE, without_relay, 0)
        write_rows(y_ref, out_ref, rest)
        sent(1, g1_ref)
        for d in range(1, HEADS_AXIS):
            peer = head_at(d, 1)
            remote(
                zsend.at[peer], zrecv1.at[head], zs_sem.at[d], zr1_sem.at[d], h=peer
            ).wait_send()

    sent(0, g0_ref)

    @pl.when(section == 0)
    def _():
        for d in range(HEADS_AXIS):
            peer = head_at(d, 1)
            remote(
                zsend.at[peer], zrecv0.at[head], zs_sem.at[d], zr0_sem.at[d], s=1, h=peer
            ).wait_send()
            if d > 0:
                remote(
                    zsend.at[peer],
                    zrecv0.at[head],
                    zs_sem.at[HEADS_AXIS + d],
                    zr0_sem.at[d],
                    h=peer,
                ).wait_send()
        remote(gain_own, gain0, gain_sem.at[0], gain_sem.at[1], s=1).wait_send()


def local(residual_incoming, norm_gain, key_states, value_states, positions):
    vmem = pl.BlockSpec(memory_space=pltpu.VMEM)
    smem = pl.BlockSpec(memory_space=pltpu.SMEM)
    dma = pltpu.SemaphoreType.DMA
    state = pltpu.VMEM((2, TILES, TILE, HEAD_DIM), F32)
    pieces = pltpu.VMEM((HEADS_AXIS, 32, HEAD_DIM), BF16)
    blocks = pltpu.VMEM((CTX, SLOT, HEAD_DIM), BF16)
    anywhere = pl.BlockSpec(memory_space=pltpu.HBM)
    rows = pltpu.VMEM((ROWS, HEAD_DIM), BF16)
    out = pl.pallas_call(
        sublayers_kernel,
        name="sublayers",
        out_shape=jax.ShapeDtypeStruct(residual_incoming.shape, BF16),
        in_specs=[anywhere, anywhere, smem, anywhere, anywhere],
        out_specs=vmem,
        scratch_shapes=[
            pltpu.VMEM(residual_incoming.shape, BF16),
            rows,
            rows,
            pieces,
            pieces,
            pieces,
            pltpu.VMEM((2, SLOT, HEAD_DIM), BF16),
            blocks,
            blocks,
            pltpu.VMEM((GROUP, HEAD_DIM), F32),
            pltpu.VMEM((GROUP, HEAD_DIM), F32),
            pltpu.VMEM((3, 8, HEAD_DIM), F32),
            pltpu.VMEM((HEADS_AXIS, 8, HEAD_DIM), F32),
            pltpu.VMEM((2, HEADS_AXIS, 8, HEAD_DIM), F32),
            pltpu.VMEM(residual_incoming.shape, BF16),
            pltpu.VMEM((2, TILES, TILE, HEAD_DIM), BF16),
            state,
            state,
            state,
            pltpu.VMEM((TILES, TILE, HEAD_DIM), jnp.int32),
            dma((2 * HEADS_AXIS,)),
            dma((HEADS_AXIS,)),
            dma((HEADS_AXIS,)),
            dma((3, HEADS_AXIS)),
            dma((3, HEADS_AXIS)),
            dma((2,)),
            dma((2, CHIPS)),
            dma((2, CHIPS)),
            dma((2, CHIPS)),
            dma((2, CHIPS)),
            dma((4,)),
        ],
        compiler_params=pltpu.CompilerParams(
            collective_id=0, has_side_effects=True, vmem_limit_bytes=62 * 2**20
        ),
    )(
        key_states.reshape(ROWS, HEAD_DIM),
        value_states.reshape(ROWS, HEAD_DIM),
        positions,
        residual_incoming,
        norm_gain.reshape(-1, HEAD_DIM),
    )
    return out[None]


def solution(mesh):
    placed = (
        P("ctx", "head"),
        P("section", None),
        P("section", ("ctx", "head"), None, None),
        P("section", ("ctx", "head"), None, None),
        P(("ctx", "head")),
    )
    return jax.shard_map(
        local, mesh=mesh, in_specs=placed, out_specs=P("section", "ctx", "head"), check_vma=False
    )
```

```python
import math

import jax
import jax.numpy as jnp
from jax import lax
from jax.experimental import pallas as pl
from jax.experimental.pallas import tpu as pltpu
from jax.sharding import PartitionSpec as P

HEAD_DIM = 128
SPAN = 48
EPSILON = 1e-05
ROWS = 2 * SPAN
SLOT = 2 * ROWS + 16
CHIPS = 16
SIDE = 4
HEADS_AXIS = 8
SECTIONS = 2
CTX = 2 * CHIPS
RUNS = 2 * CTX
PIECE = ROWS // HEADS_AXIS
WAVE = 2 * SIDE
TOKENS = 16
TILE = 16 * TOKENS
TILES = SPAN // TOKENS
GROUP = 16
SCALE = math.log2(math.e) / math.sqrt(HEAD_DIM)
SECOND_AFTER = 1
ORDER = tuple(SIDE * dx + dy for dx in range(SIDE) for dy in (1, 3, 2, 0) if dx + dy > 0)
F32 = jnp.float32
BF16 = jnp.bfloat16


def iota(shape, dim):
    return lax.broadcasted_iota(jnp.int32, shape, dim)


def first_run_of(pos_ref, head):
    run = pos_ref[0] // SPAN
    return jnp.where(head * PIECE < SPAN, run, RUNS - 1 - run)


def square_rows(wide_tiles):
    total = wide_tiles[0] * wide_tiles[0]
    for tile in wide_tiles[1:]:
        total = total + tile * tile
    padded = jnp.concatenate([total, jnp.zeros((HEAD_DIM - ROWS, HEAD_DIM), F32)], axis=0)
    turned = padded.T
    part = turned[0:8]
    for k in range(1, HEAD_DIM // 8):
        part = part + turned[8 * k : 8 * k + 8]
    return part


def column_scale(parts):
    total = parts[0]
    for d in range(1, HEADS_AXIS):
        total = total + parts[d]
    total = jnp.sum(total, axis=0, keepdims=True)
    scale = lax.rsqrt(total * (1.0 / (HEADS_AXIS * GROUP * HEAD_DIM)) + EPSILON)
    return jnp.broadcast_to(scale, (HEAD_DIM, HEAD_DIM)).T


def update(q, k, v, old, gap, place):
    s = lax.dot_general(q, k, (((1,), (1,)), ((), ())), preferred_element_type=F32)
    parts = s.shape[1] // HEAD_DIM
    s = jnp.where(gap <= jnp.concatenate([place] * parts, axis=1), s, -1e30)
    new = jnp.maximum(old[0], jnp.max(s, axis=1, keepdims=True))
    p = jnp.exp2((s - jnp.concatenate([new] * parts, axis=1)) * SCALE)
    both = jnp.dot(p.astype(BF16), v, preferred_element_type=F32)
    factor = jnp.exp2((old[0] - new) * SCALE)
    return new, old[1] * factor + both[:, HEAD_DIM:], old[2] * factor + both[:, :HEAD_DIM]


def sublayers_kernel(
    k_ref,
    v_ref,
    pos_ref,
    x_hbm,
    gain_ref,
    out_ref,
    x_ref,
    k_own,
    v_own,
    zsend,
    zrecv0,
    zrecv1,
    stage,
    g0_ref,
    g1_ref,
    gain0,
    gain_own,
    sq_own,
    sq0,
    sq1,
    y_ref,
    q_ref,
    m_ref,
    l_ref,
    acc_ref,
    place_ref,
    zs_sem,
    zr0_sem,
    zr1_sem,
    sqs_sem,
    sqr_sem,
    gain_sem,
    gs_sem,
    gr_sem,
    fs_sem,
    fr_sem,
    in_sem,
):
    section = lax.axis_index("section")
    ctx = lax.axis_index("ctx")
    head = lax.axis_index("head")
    chip = ctx // 2
    core = ctx % 2
    cx = chip // SIDE
    cy = chip % SIDE
    sibling = ctx + 1 - 2 * core

    def at(offset, sign):
        dx, dy = offset // SIDE, offset % SIDE
        px = lax.rem(cx + sign * dx + SIDE, SIDE)
        py = lax.rem(cy + sign * dy + SIDE, SIDE)
        return (px * SIDE + py) * 2 + core

    def head_at(offset, sign):
        return lax.rem(head + sign * offset + HEADS_AXIS, HEADS_AXIS)

    def remote(src, dst, send, recv, s=None, c=None, h=None):
        target = (
            section if s is None else s,
            ctx if c is None else c,
            head if h is None else h,
        )
        return pltpu.make_async_remote_copy(
            src_ref=src,
            dst_ref=dst,
            send_sem=send,
            recv_sem=recv,
            device_id=target,
            device_id_type=pl.DeviceIdType.MESH,
        )

    own_rows = pl.ds(pl.multiple_of(head * GROUP, GROUP), GROUP)
    fetches = [
        pltpu.make_async_copy(src, dst, in_sem.at[i])
        for i, (src, dst) in enumerate(
            (
                (k_ref, k_own),
                (v_ref, v_own),
                (x_hbm, x_ref),
                (gain_ref.at[own_rows], gain_own),
            )
        )
    ]
    for fetch in fetches:
        fetch.start()

    barrier = pltpu.get_barrier_semaphore()

    def greet(s, c, h):
        pl.semaphore_signal(
            barrier, inc=1, device_id=(s, c, h), device_id_type=pl.DeviceIdType.MESH
        )

    @pl.when(section == 1)
    def _():
        for d in range(HEADS_AXIS):
            greet(0, ctx, head_at(d, 1))

    for d in range(1, HEADS_AXIS):
        greet(section, ctx, head_at(d, 1))
    for d in range(1, CHIPS):
        greet(section, at(d, 1), head)
    greet(section, sibling, head)

    out_row = iota((HEAD_DIM, ROWS), 0)
    in_row = iota((HEAD_DIM, ROWS), 1)
    pick = (out_row % 16) * HEADS_AXIS + out_row // 16
    spread = jnp.where((in_row == pick) & (out_row % 16 < PIECE), 1.0, 0.0).astype(BF16)
    fetches[0].wait()
    fetches[1].wait()
    keys = jnp.dot(spread, k_own[...], preferred_element_type=F32).astype(BF16)
    values = jnp.dot(spread, v_own[...], preferred_element_type=F32).astype(BF16)
    for h in range(HEADS_AXIS):
        zsend[h, 0:16] = keys[16 * h : 16 * h + 16]
        zsend[h, 16:32] = values[16 * h : 16 * h + 16]
    first_run = first_run_of(pos_ref, head)
    swap = first_run >= CTX
    low = jnp.where(swap, RUNS - 1 - first_run, first_run)

    @pl.when(section == 0)
    def _():
        pl.semaphore_wait(barrier, 2 * HEADS_AXIS - 1 + CHIPS)
        for d in range(HEADS_AXIS):
            peer = head_at(d, 1)
            remote(
                zsend.at[peer],
                zrecv0.at[head],
                zs_sem.at[d],
                zr0_sem.at[d],
                s=1,
                h=peer,
            ).start()
            if d > 0:
                remote(
                    zsend.at[peer],
                    zrecv0.at[head],
                    zs_sem.at[HEADS_AXIS + d],
                    zr0_sem.at[d],
                    h=peer,
                ).start()
        zrecv0[head] = zsend[head]

    @pl.when(section == 1)
    def _():
        pl.semaphore_wait(barrier, HEADS_AXIS - 1 + CHIPS)
        for d in range(1, HEADS_AXIS):
            peer = head_at(d, 1)
            remote(
                zsend.at[peer],
                zrecv1.at[head],
                zs_sem.at[d],
                zr1_sem.at[d],
                h=peer,
            ).start()
        zrecv1[head] = zsend[head]

    def send_sums(part, sq):
        for d in range(1, HEADS_AXIS):
            remote(
                sq_own.at[part],
                sq.at[head],
                sqs_sem.at[part, d],
                sqr_sem.at[part, d],
                h=head_at(d, 1),
            ).start()

    def finish_sums(part, sq):
        for d in range(1, HEADS_AXIS):
            remote(
                sq_own.at[part],
                sq.at[head_at(d, -1)],
                sqs_sem.at[part, d],
                sqr_sem.at[part, d],
                h=head_at(d, 1),
            ).wait()

    fetches[2].wait()
    fetches[3].wait()
    sq_own[0] = square_rows(
        [x_ref[:, HEAD_DIM * a : HEAD_DIM * (a + 1)].astype(F32) for a in range(GROUP)]
    )
    sq0[head] = sq_own[0]
    send_sums(0, sq0)

    @pl.when(section == 0)
    def _():
        remote(gain_own, gain0, gain_sem.at[0], gain_sem.at[1], s=1).start()
        gain0[...] = gain_own[...]

    row = iota((2 * ROWS, 16 * 16), 0)
    col = iota((2 * ROWS, 16 * 16), 1)
    turn = jnp.where(swap, SPAN, 0)
    place = lax.rem(row + turn, ROWS)
    source = (place // PIECE) * 32 + place % PIECE + jnp.where(row >= ROWS, 16, 0)
    compact = jnp.where(col == source, 1.0, 0.0).astype(BF16)
    meta = (jnp.zeros((16, HEAD_DIM), F32) + low.astype(F32)).astype(BF16)

    def begin_layer(layer, zrecv, g_ref):
        pieces = zrecv[...].reshape(16 * 16, HEAD_DIM)
        block = jnp.dot(compact, pieces, preferred_element_type=F32).astype(BF16)
        stage[layer, 0 : 2 * ROWS] = block
        stage[layer, 2 * ROWS : SLOT] = meta
        remote(
            stage.at[layer],
            g_ref.at[ctx],
            fs_sem.at[layer, 0],
            fr_sem.at[layer, 0],
            c=sibling,
        ).start()
        for d in ORDER:
            remote(
                stage.at[layer],
                g_ref.at[ctx],
                gs_sem.at[layer, d],
                gr_sem.at[layer, d],
                c=at(d, 1),
            ).start()
        g_ref[ctx, 0 : 2 * ROWS] = block
        g_ref[ctx, 2 * ROWS : SLOT] = meta

    def relay(layer, g_ref, d):
        got = at(d, -1)
        remote(
            stage.at[layer],
            g_ref.at[got],
            gs_sem.at[layer, d],
            gr_sem.at[layer, d],
            c=at(d, 1),
        ).wait_recv()
        remote(
            g_ref.at[got],
            g_ref.at[got],
            fs_sem.at[layer, d],
            fr_sem.at[layer, d],
            c=sibling,
        ).start()

    def relayed(layer, g_ref, d, own=False):
        slot = at(d, -1) + 1 - 2 * core
        mine = stage.at[layer] if own else g_ref.at[at(d, -1)]
        remote(
            mine, g_ref.at[slot], fs_sem.at[layer, d], fr_sem.at[layer, d], c=sibling
        ).wait_recv()

    def sent(layer, g_ref):
        for d in range(CHIPS):
            if d > 0:
                remote(
                    stage.at[layer],
                    g_ref.at[ctx],
                    gs_sem.at[layer, d],
                    gr_sem.at[layer, d],
                    c=at(d, 1),
                ).wait_send()
            mine = stage.at[layer] if d == 0 else g_ref.at[at(d, -1)]
            remote(
                mine, g_ref.at[ctx], fs_sem.at[layer, d], fr_sem.at[layer, d], c=sibling
            ).wait_send()

    @pl.when(section == 1)
    def _():
        remote(
            zsend.at[head], zrecv0.at[head], zs_sem.at[0], zr0_sem.at[0], s=0
        ).wait_recv()

    for d in range(1, HEADS_AXIS):
        got = head_at(d, -1)
        remote(
            zsend.at[got], zrecv0.at[got], zs_sem.at[d], zr0_sem.at[d], h=got
        ).wait_recv()
    begin_layer(0, zrecv0, g0_ref)

    def clear_state():
        m_ref[...] = jnp.full(m_ref.shape, -1e30, F32)
        l_ref[...] = jnp.zeros(l_ref.shape, F32)
        acc_ref[...] = jnp.zeros(acc_ref.shape, F32)

    clear_state()
    place_shape = (TILES, TILE, HEAD_DIM)
    place_ref[...] = iota(place_shape, 0) * TOKENS + iota(place_shape, 1) % TOKENS

    def make_queries(h_ref, sq, gain, tiles):
        column = column_scale([sq[d] for d in range(HEADS_AXIS)])
        for tile in tiles:
            for a in range(GROUP):
                cols = slice(HEAD_DIM * a, HEAD_DIM * (a + 1))
                qs = []
                for half in range(2):
                    rows = slice(half * SPAN + tile * TOKENS, half * SPAN + (tile + 1) * TOKENS)
                    wide = h_ref[rows, cols].astype(F32)
                    qs.append(wide * column[rows] * gain[a : a + 1, :])
                to = slice(TOKENS * a, TOKENS * (a + 1))
                q_ref[0, tile, to, :] = jnp.where(swap, qs[1], qs[0]).astype(BF16)
                q_ref[1, tile, to, :] = jnp.where(swap, qs[0], qs[1]).astype(BF16)

    def flat(ref, kind, tiles):
        rows = ref[kind, tiles.start : tiles.stop]
        return rows.reshape(len(tiles) * TILE, HEAD_DIM)

    def update_rows(kind, tiles, k, v, gap):
        old = tuple(flat(ref, kind, tiles) for ref in (m_ref, l_ref, acc_ref))
        place = place_ref[tiles.start : tiles.stop].reshape(len(tiles) * TILE, HEAD_DIM)
        state = update(flat(q_ref, kind, tiles), k, v, old, gap, place)
        for ref, part in zip((m_ref, l_ref, acc_ref), state):
            ref[kind, tiles.start : tiles.stop] = part.reshape(len(tiles), TILE, HEAD_DIM)

    def attend_wave(g_ref, dx, tiles):
        row_of = lax.rem(cx - dx + SIDE, SIDE)
        here = pl.ds(row_of * WAVE, WAVE)
        size = 2 * WAVE * SPAN
        lane = iota((1, size), 1)
        tag = jnp.zeros((1, size), F32)
        tags = g_ref[here, 2 * ROWS : SLOT, :].astype(F32)
        for i in range(WAVE):
            wide = jnp.concatenate([tags[i, 0:1, :]] * (size // HEAD_DIM), axis=1)
            tag = jnp.where(lane // ROWS == i, wide, tag)
        at_row = lane % ROWS
        run = tag.astype(jnp.int32)
        run = jnp.where(at_row >= SPAN, RUNS - 1 - run, run)
        key_pos = run * SPAN + at_row % SPAN
        low_lane = iota((1, size // 2), 1)
        tag = jnp.zeros((1, size // 2), F32)
        for i in range(WAVE):
            wide = jnp.concatenate([tags[i, 0:1, :]] * (size // 2 // HEAD_DIM), axis=1)
            tag = jnp.where(low_lane // SPAN == i, wide, tag)
        low_pos = tag.astype(jnp.int32) * SPAN + low_lane % SPAN
        k = g_ref[here, 0:ROWS, :].reshape(size, HEAD_DIM)
        v = g_ref[here, ROWS : 2 * ROWS, :].reshape(size, HEAD_DIM)
        k_low = g_ref[here, 0:SPAN, :].reshape(size // 2, HEAD_DIM)
        v_low = g_ref[here, ROWS : ROWS + SPAN, :].reshape(size // 2, HEAD_DIM)
        ones = jnp.ones((size, HEAD_DIM), BF16)
        v = jnp.concatenate([v, ones], axis=1)
        v_low = jnp.concatenate([v_low, ones[: size // 2]], axis=1)
        update_rows(1, tiles, k, v, key_pos - (RUNS - 1 - low) * SPAN)
        update_rows(0, tiles, k_low, v_low, low_pos - low * SPAN)

    def write_rows(h_ref, to_ref, tiles):
        for tile in tiles:
            mixed = []
            for kind in range(2):
                mixed.append(acc_ref[kind, tile] / l_ref[kind, tile])
            halves = (
                jnp.where(swap, mixed[1], mixed[0]).astype(BF16).astype(F32),
                jnp.where(swap, mixed[0], mixed[1]).astype(BF16).astype(F32),
            )
            for half in range(2):
                r0 = half * SPAN + tile * TOKENS
                rows = slice(r0, r0 + TOKENS)
                for a in range(GROUP):
                    cols = slice(HEAD_DIM * a, HEAD_DIM * (a + 1))
                    part = halves[half][TOKENS * a : TOKENS * (a + 1)]
                    to_ref[rows, cols] = (h_ref[rows, cols].astype(F32) + part).astype(BF16)

    def relay_wave(layer, g_ref, dx):
        @pl.when(dx > 0)
        def _():
            relay(layer, g_ref, dx * SIDE)

        for dy in range(1, SIDE):
            relay(layer, g_ref, dx * SIDE + dy)

    def relayed_wave(layer, g_ref, dx):
        @pl.when(dx == 0)
        def _():
            relayed(layer, g_ref, 0, True)

        @pl.when(dx > 0)
        def _():
            relayed(layer, g_ref, dx * SIDE)

        for dy in range(1, SIDE):
            relayed(layer, g_ref, dx * SIDE + dy)

    finish_sums(0, sq0)

    @pl.when(section == 1)
    def _():
        remote(gain_own, gain0, gain_sem.at[0], gain_sem.at[1], s=0).wait_recv()
        for d in range(1, HEADS_AXIS):
            got = head_at(d, -1)
            remote(
                zsend.at[got], zrecv1.at[got], zs_sem.at[d], zr1_sem.at[d], h=got
            ).wait_recv()

    every = range(TILES)
    make_queries(x_ref, sq0, gain0, every)

    def early(dx, carry):
        relay_wave(0, g0_ref, dx + 1)

        @pl.when((section == 1) & (dx == SECOND_AFTER))
        def _():
            begin_layer(1, zrecv1, g1_ref)

        relayed_wave(0, g0_ref, dx)
        attend_wave(g0_ref, dx, every)
        return carry

    relay_wave(0, g0_ref, jnp.int32(0))
    lax.fori_loop(0, SIDE - 1, early, 0)

    first, rest = range(0, 1), range(1, TILES)

    def squares_of(part, sq):
        sq_own[part] = square_rows(
            [y_ref[:, HEAD_DIM * a : HEAD_DIM * (a + 1)].astype(F32) for a in range(GROUP)]
        )
        sq[head] = sq_own[part]
        send_sums(part, sq)

    y_ref[...] = x_ref[...]
    relayed_wave(0, g0_ref, jnp.int32(SIDE - 1))
    attend_wave(g0_ref, SIDE - 1, first)
    write_rows(x_ref, y_ref, first)

    @pl.when(section == 1)
    def _():
        squares_of(1, sq1.at[0])

    attend_wave(g0_ref, SIDE - 1, rest)
    write_rows(x_ref, y_ref, rest)

    @pl.when(section == 0)
    def _():
        out_ref[...] = y_ref[...]

    @pl.when(section == 1)
    def _():
        squares_of(2, sq1.at[1])
        clear_state()
        relay_wave(1, g1_ref, jnp.int32(0))
        sent(0, g0_ref)
        for d in range(1, HEADS_AXIS):
            peer = head_at(d, 1)
            remote(
                zsend.at[peer], zrecv1.at[head], zs_sem.at[d], zr1_sem.at[d], h=peer
            ).wait_send()
        relay_wave(1, g1_ref, jnp.int32(1))
        finish_sums(1, sq1.at[0])
        make_queries(y_ref, sq1.at[0], gain_own, first)

        def with_relay(dx, carry):
            @pl.when(dx < SIDE - 2)
            def _():
                relay_wave(1, g1_ref, dx + 2)

            relayed_wave(1, g1_ref, dx)
            attend_wave(g1_ref, dx, first)
            return carry

        lax.fori_loop(0, SIDE, with_relay, 0)
        write_rows(y_ref, out_ref, first)
        sent(1, g1_ref)
        finish_sums(2, sq1.at[1])
        make_queries(y_ref, sq1.at[1], gain_own, rest)

        def without_relay(dx, carry):
            attend_wave(g1_ref, dx, rest)
            return carry

        lax.fori_loop(0, SIDE, without_relay, 0)
        write_rows(y_ref, out_ref, rest)

    @pl.when(section == 0)
    def _():
        sent(0, g0_ref)
        for d in range(HEADS_AXIS):
            peer = head_at(d, 1)
            remote(
                zsend.at[peer], zrecv0.at[head], zs_sem.at[d], zr0_sem.at[d], s=1, h=peer
            ).wait_send()
            if d > 0:
                remote(
                    zsend.at[peer],
                    zrecv0.at[head],
                    zs_sem.at[HEADS_AXIS + d],
                    zr0_sem.at[d],
                    h=peer,
                ).wait_send()
        remote(gain_own, gain0, gain_sem.at[0], gain_sem.at[1], s=1).wait_send()


def local(residual_incoming, norm_gain, key_states, value_states, positions):
    vmem = pl.BlockSpec(memory_space=pltpu.VMEM)
    smem = pl.BlockSpec(memory_space=pltpu.SMEM)
    dma = pltpu.SemaphoreType.DMA
    state = pltpu.VMEM((2, TILES, TILE, HEAD_DIM), F32)
    pieces = pltpu.VMEM((HEADS_AXIS, 32, HEAD_DIM), BF16)
    blocks = pltpu.VMEM((CTX, SLOT, HEAD_DIM), BF16)
    anywhere = pl.BlockSpec(memory_space=pltpu.HBM)
    rows = pltpu.VMEM((ROWS, HEAD_DIM), BF16)
    out = pl.pallas_call(
        sublayers_kernel,
        name="sublayers",
        out_shape=jax.ShapeDtypeStruct(residual_incoming.shape, BF16),
        in_specs=[anywhere, anywhere, smem, anywhere, anywhere],
        out_specs=vmem,
        scratch_shapes=[
            pltpu.VMEM(residual_incoming.shape, BF16),
            rows,
            rows,
            pieces,
            pieces,
            pieces,
            pltpu.VMEM((2, SLOT, HEAD_DIM), BF16),
            blocks,
            blocks,
            pltpu.VMEM((GROUP, HEAD_DIM), F32),
            pltpu.VMEM((GROUP, HEAD_DIM), F32),
            pltpu.VMEM((3, 8, HEAD_DIM), F32),
            pltpu.VMEM((HEADS_AXIS, 8, HEAD_DIM), F32),
            pltpu.VMEM((2, HEADS_AXIS, 8, HEAD_DIM), F32),
            pltpu.VMEM(residual_incoming.shape, BF16),
            pltpu.VMEM((2, TILES, TILE, HEAD_DIM), BF16),
            state,
            state,
            state,
            pltpu.VMEM((TILES, TILE, HEAD_DIM), jnp.int32),
            dma((2 * HEADS_AXIS,)),
            dma((HEADS_AXIS,)),
            dma((HEADS_AXIS,)),
            dma((3, HEADS_AXIS)),
            dma((3, HEADS_AXIS)),
            dma((2,)),
            dma((2, CHIPS)),
            dma((2, CHIPS)),
            dma((2, CHIPS)),
            dma((2, CHIPS)),
            dma((4,)),
        ],
        compiler_params=pltpu.CompilerParams(
            collective_id=0, has_side_effects=True, vmem_limit_bytes=62 * 2**20
        ),
    )(
        key_states.reshape(ROWS, HEAD_DIM),
        value_states.reshape(ROWS, HEAD_DIM),
        positions,
        residual_incoming,
        norm_gain.reshape(-1, HEAD_DIM),
    )
    return out[None]


def solution(mesh):
    placed = (
        P("ctx", "head"),
        P("section", None),
        P("section", ("ctx", "head"), None, None),
        P("section", ("ctx", "head"), None, None),
        P(("ctx", "head")),
    )
    return jax.shard_map(
        local, mesh=mesh, in_specs=placed, out_specs=P("section", "ctx", "head"), check_vma=False
    )
```

```python
import math

import jax
import jax.numpy as jnp
from jax import lax
from jax.experimental import pallas as pl
from jax.experimental.pallas import tpu as pltpu
from jax.sharding import PartitionSpec as P

HEAD_DIM = 128
SPAN = 48
EPSILON = 1e-05
ROWS = 2 * SPAN
SLOT = 2 * ROWS + 16
CHIPS = 16
SIDE = 4
HEADS_AXIS = 8
SECTIONS = 2
CTX = 2 * CHIPS
RUNS = 2 * CTX
PIECE = ROWS // HEADS_AXIS
WAVE = 2 * SIDE
TOKENS = 16
TILE = 16 * TOKENS
TILES = SPAN // TOKENS
GROUP = 16
SCALE = math.log2(math.e) / math.sqrt(HEAD_DIM)
SECOND_AFTER = 0
ORDER = tuple(SIDE * dx + dy for dx in range(SIDE) for dy in (1, 3, 2, 0) if dx + dy > 0)
F32 = jnp.float32
BF16 = jnp.bfloat16


def iota(shape, dim):
    return lax.broadcasted_iota(jnp.int32, shape, dim)


def first_run_of(pos_ref, head):
    run = pos_ref[0] // SPAN
    return jnp.where(head * PIECE < SPAN, run, RUNS - 1 - run)


def square_rows(wide_tiles):
    total = wide_tiles[0] * wide_tiles[0]
    for tile in wide_tiles[1:]:
        total = total + tile * tile
    padded = jnp.concatenate([total, jnp.zeros((HEAD_DIM - ROWS, HEAD_DIM), F32)], axis=0)
    turned = padded.T
    part = turned[0:8]
    for k in range(1, HEAD_DIM // 8):
        part = part + turned[8 * k : 8 * k + 8]
    return part


def column_scale(parts):
    total = parts[0]
    for d in range(1, HEADS_AXIS):
        total = total + parts[d]
    total = jnp.sum(total, axis=0, keepdims=True)
    scale = lax.rsqrt(total * (1.0 / (HEADS_AXIS * GROUP * HEAD_DIM)) + EPSILON)
    return jnp.broadcast_to(scale, (HEAD_DIM, HEAD_DIM)).T


def update(q, k, v, old, gap, place):
    s = lax.dot_general(q, k, (((1,), (1,)), ((), ())), preferred_element_type=F32)
    parts = s.shape[1] // HEAD_DIM
    s = jnp.where(gap <= jnp.concatenate([place] * parts, axis=1), s, -1e30)
    new = jnp.maximum(old[0], jnp.max(s, axis=1, keepdims=True))
    p = jnp.exp2((s - jnp.concatenate([new] * parts, axis=1)) * SCALE)
    both = jnp.dot(p.astype(BF16), v, preferred_element_type=F32)
    factor = jnp.exp2((old[0] - new) * SCALE)
    return new, old[1] * factor + both[:, HEAD_DIM:], old[2] * factor + both[:, :HEAD_DIM]


def sublayers_kernel(
    k_ref,
    v_ref,
    pos_ref,
    x_hbm,
    gain_ref,
    out_ref,
    x_ref,
    k_own,
    v_own,
    zsend,
    zrecv0,
    zrecv1,
    stage,
    g0_ref,
    g1_ref,
    gain0,
    gain_own,
    sq_own,
    sq0,
    sq1,
    y_ref,
    q_ref,
    m_ref,
    l_ref,
    acc_ref,
    place_ref,
    zs_sem,
    zr0_sem,
    zr1_sem,
    sqs_sem,
    sqr_sem,
    gain_sem,
    gs_sem,
    gr_sem,
    fs_sem,
    fr_sem,
    in_sem,
):
    section = lax.axis_index("section")
    ctx = lax.axis_index("ctx")
    head = lax.axis_index("head")
    chip = ctx // 2
    core = ctx % 2
    cx = chip // SIDE
    cy = chip % SIDE
    sibling = ctx + 1 - 2 * core

    def at(offset, sign):
        dx, dy = offset // SIDE, offset % SIDE
        px = lax.rem(cx + sign * dx + SIDE, SIDE)
        py = lax.rem(cy + sign * dy + SIDE, SIDE)
        return (px * SIDE + py) * 2 + core

    def head_at(offset, sign):
        return lax.rem(head + sign * offset + HEADS_AXIS, HEADS_AXIS)

    def remote(src, dst, send, recv, s=None, c=None, h=None):
        target = (
            section if s is None else s,
            ctx if c is None else c,
            head if h is None else h,
        )
        return pltpu.make_async_remote_copy(
            src_ref=src,
            dst_ref=dst,
            send_sem=send,
            recv_sem=recv,
            device_id=target,
            device_id_type=pl.DeviceIdType.MESH,
        )

    own_rows = pl.ds(pl.multiple_of(head * GROUP, GROUP), GROUP)
    fetches = [
        pltpu.make_async_copy(src, dst, in_sem.at[i])
        for i, (src, dst) in enumerate(
            (
                (k_ref, k_own),
                (v_ref, v_own),
                (x_hbm, x_ref),
                (gain_ref.at[own_rows], gain_own),
            )
        )
    ]
    for fetch in fetches:
        fetch.start()

    barrier = pltpu.get_barrier_semaphore()

    def greet(s, c, h):
        pl.semaphore_signal(
            barrier, inc=1, device_id=(s, c, h), device_id_type=pl.DeviceIdType.MESH
        )

    @pl.when(section == 1)
    def _():
        for d in range(HEADS_AXIS):
            greet(0, ctx, head_at(d, 1))

    for d in range(1, HEADS_AXIS):
        greet(section, ctx, head_at(d, 1))
    for d in range(1, CHIPS):
        greet(section, at(d, 1), head)
    greet(section, sibling, head)

    out_row = iota((HEAD_DIM, ROWS), 0)
    in_row = iota((HEAD_DIM, ROWS), 1)
    pick = (out_row % 16) * HEADS_AXIS + out_row // 16
    spread = jnp.where((in_row == pick) & (out_row % 16 < PIECE), 1.0, 0.0).astype(BF16)
    fetches[0].wait()
    fetches[1].wait()
    keys = jnp.dot(spread, k_own[...], preferred_element_type=F32).astype(BF16)
    values = jnp.dot(spread, v_own[...], preferred_element_type=F32).astype(BF16)
    for h in range(HEADS_AXIS):
        zsend[h, 0:16] = keys[16 * h : 16 * h + 16]
        zsend[h, 16:32] = values[16 * h : 16 * h + 16]
    first_run = first_run_of(pos_ref, head)
    swap = first_run >= CTX
    low = jnp.where(swap, RUNS - 1 - first_run, first_run)

    @pl.when(section == 0)
    def _():
        pl.semaphore_wait(barrier, 2 * HEADS_AXIS - 1 + CHIPS)
        for d in range(HEADS_AXIS):
            peer = head_at(d, 1)
            remote(
                zsend.at[peer],
                zrecv0.at[head],
                zs_sem.at[d],
                zr0_sem.at[d],
                s=1,
                h=peer,
            ).start()
            if d > 0:
                remote(
                    zsend.at[peer],
                    zrecv0.at[head],
                    zs_sem.at[HEADS_AXIS + d],
                    zr0_sem.at[d],
                    h=peer,
                ).start()
        zrecv0[head] = zsend[head]

    @pl.when(section == 1)
    def _():
        pl.semaphore_wait(barrier, HEADS_AXIS - 1 + CHIPS)
        for d in range(1, HEADS_AXIS):
            peer = head_at(d, 1)
            remote(
                zsend.at[peer],
                zrecv1.at[head],
                zs_sem.at[d],
                zr1_sem.at[d],
                h=peer,
            ).start()
        zrecv1[head] = zsend[head]

    def send_sums(part, sq):
        for d in range(1, HEADS_AXIS):
            remote(
                sq_own.at[part],
                sq.at[head],
                sqs_sem.at[part, d],
                sqr_sem.at[part, d],
                h=head_at(d, 1),
            ).start()

    def finish_sums(part, sq):
        for d in range(1, HEADS_AXIS):
            remote(
                sq_own.at[part],
                sq.at[head_at(d, -1)],
                sqs_sem.at[part, d],
                sqr_sem.at[part, d],
                h=head_at(d, 1),
            ).wait()

    fetches[2].wait()
    fetches[3].wait()
    sq_own[0] = square_rows(
        [x_ref[:, HEAD_DIM * a : HEAD_DIM * (a + 1)].astype(F32) for a in range(GROUP)]
    )
    sq0[head] = sq_own[0]
    send_sums(0, sq0)

    @pl.when(section == 0)
    def _():
        remote(gain_own, gain0, gain_sem.at[0], gain_sem.at[1], s=1).start()
        gain0[...] = gain_own[...]

    row = iota((2 * ROWS, 16 * 16), 0)
    col = iota((2 * ROWS, 16 * 16), 1)
    turn = jnp.where(swap, SPAN, 0)
    place = lax.rem(row + turn, ROWS)
    source = (place // PIECE) * 32 + place % PIECE + jnp.where(row >= ROWS, 16, 0)
    compact = jnp.where(col == source, 1.0, 0.0).astype(BF16)
    meta = (jnp.zeros((16, HEAD_DIM), F32) + low.astype(F32)).astype(BF16)

    def begin_layer(layer, zrecv, g_ref):
        pieces = zrecv[...].reshape(16 * 16, HEAD_DIM)
        block = jnp.dot(compact, pieces, preferred_element_type=F32).astype(BF16)
        stage[layer, 0 : 2 * ROWS] = block
        stage[layer, 2 * ROWS : SLOT] = meta
        remote(
            stage.at[layer],
            g_ref.at[ctx],
            fs_sem.at[layer, 0],
            fr_sem.at[layer, 0],
            c=sibling,
        ).start()
        for d in ORDER:
            remote(
                stage.at[layer],
                g_ref.at[ctx],
                gs_sem.at[layer, d],
                gr_sem.at[layer, d],
                c=at(d, 1),
            ).start()
        g_ref[ctx, 0 : 2 * ROWS] = block
        g_ref[ctx, 2 * ROWS : SLOT] = meta

    def relay(layer, g_ref, d):
        got = at(d, -1)
        remote(
            stage.at[layer],
            g_ref.at[got],
            gs_sem.at[layer, d],
            gr_sem.at[layer, d],
            c=at(d, 1),
        ).wait_recv()
        remote(
            g_ref.at[got],
            g_ref.at[got],
            fs_sem.at[layer, d],
            fr_sem.at[layer, d],
            c=sibling,
        ).start()

    def relayed(layer, g_ref, d, own=False):
        slot = at(d, -1) + 1 - 2 * core
        mine = stage.at[layer] if own else g_ref.at[at(d, -1)]
        remote(
            mine, g_ref.at[slot], fs_sem.at[layer, d], fr_sem.at[layer, d], c=sibling
        ).wait_recv()

    def sent(layer, g_ref):
        for d in range(CHIPS):
            if d > 0:
                remote(
                    stage.at[layer],
                    g_ref.at[ctx],
                    gs_sem.at[layer, d],
                    gr_sem.at[layer, d],
                    c=at(d, 1),
                ).wait_send()
            mine = stage.at[layer] if d == 0 else g_ref.at[at(d, -1)]
            remote(
                mine, g_ref.at[ctx], fs_sem.at[layer, d], fr_sem.at[layer, d], c=sibling
            ).wait_send()

    @pl.when(section == 1)
    def _():
        remote(
            zsend.at[head], zrecv0.at[head], zs_sem.at[0], zr0_sem.at[0], s=0
        ).wait_recv()

    for d in range(1, HEADS_AXIS):
        got = head_at(d, -1)
        remote(
            zsend.at[got], zrecv0.at[got], zs_sem.at[d], zr0_sem.at[d], h=got
        ).wait_recv()
    begin_layer(0, zrecv0, g0_ref)

    def clear_state():
        m_ref[...] = jnp.full(m_ref.shape, -1e30, F32)
        l_ref[...] = jnp.zeros(l_ref.shape, F32)
        acc_ref[...] = jnp.zeros(acc_ref.shape, F32)

    clear_state()
    place_shape = (TILES, TILE, HEAD_DIM)
    place_ref[...] = iota(place_shape, 0) * TOKENS + iota(place_shape, 1) % TOKENS

    def make_queries(h_ref, sq, gain, tiles):
        column = column_scale([sq[d] for d in range(HEADS_AXIS)])
        for tile in tiles:
            for a in range(GROUP):
                cols = slice(HEAD_DIM * a, HEAD_DIM * (a + 1))
                qs = []
                for half in range(2):
                    rows = slice(half * SPAN + tile * TOKENS, half * SPAN + (tile + 1) * TOKENS)
                    wide = h_ref[rows, cols].astype(F32)
                    qs.append(wide * column[rows] * gain[a : a + 1, :])
                to = slice(TOKENS * a, TOKENS * (a + 1))
                q_ref[0, tile, to, :] = jnp.where(swap, qs[1], qs[0]).astype(BF16)
                q_ref[1, tile, to, :] = jnp.where(swap, qs[0], qs[1]).astype(BF16)

    def flat(ref, kind, tiles):
        rows = ref[kind, tiles.start : tiles.stop]
        return rows.reshape(len(tiles) * TILE, HEAD_DIM)

    def update_rows(kind, tiles, k, v, gap):
        old = tuple(flat(ref, kind, tiles) for ref in (m_ref, l_ref, acc_ref))
        place = place_ref[tiles.start : tiles.stop].reshape(len(tiles) * TILE, HEAD_DIM)
        state = update(flat(q_ref, kind, tiles), k, v, old, gap, place)
        for ref, part in zip((m_ref, l_ref, acc_ref), state):
            ref[kind, tiles.start : tiles.stop] = part.reshape(len(tiles), TILE, HEAD_DIM)

    def attend_wave(g_ref, dx, tiles):
        row_of = lax.rem(cx - dx + SIDE, SIDE)
        here = pl.ds(row_of * WAVE, WAVE)
        size = 2 * WAVE * SPAN
        lane = iota((1, size), 1)
        tag = jnp.zeros((1, size), F32)
        tags = g_ref[here, 2 * ROWS : SLOT, :].astype(F32)
        for i in range(WAVE):
            wide = jnp.concatenate([tags[i, 0:1, :]] * (size // HEAD_DIM), axis=1)
            tag = jnp.where(lane // ROWS == i, wide, tag)
        at_row = lane % ROWS
        run = tag.astype(jnp.int32)
        run = jnp.where(at_row >= SPAN, RUNS - 1 - run, run)
        key_pos = run * SPAN + at_row % SPAN
        low_lane = iota((1, size // 2), 1)
        tag = jnp.zeros((1, size // 2), F32)
        for i in range(WAVE):
            wide = jnp.concatenate([tags[i, 0:1, :]] * (size // 2 // HEAD_DIM), axis=1)
            tag = jnp.where(low_lane // SPAN == i, wide, tag)
        low_pos = tag.astype(jnp.int32) * SPAN + low_lane % SPAN
        k = g_ref[here, 0:ROWS, :].reshape(size, HEAD_DIM)
        v = g_ref[here, ROWS : 2 * ROWS, :].reshape(size, HEAD_DIM)
        k_low = g_ref[here, 0:SPAN, :].reshape(size // 2, HEAD_DIM)
        v_low = g_ref[here, ROWS : ROWS + SPAN, :].reshape(size // 2, HEAD_DIM)
        ones = jnp.ones((size, HEAD_DIM), BF16)
        v = jnp.concatenate([v, ones], axis=1)
        v_low = jnp.concatenate([v_low, ones[: size // 2]], axis=1)
        update_rows(1, tiles, k, v, key_pos - (RUNS - 1 - low) * SPAN)
        update_rows(0, tiles, k_low, v_low, low_pos - low * SPAN)

    def write_rows(h_ref, to_ref, tiles):
        for tile in tiles:
            mixed = []
            for kind in range(2):
                mixed.append(acc_ref[kind, tile] / l_ref[kind, tile])
            halves = (
                jnp.where(swap, mixed[1], mixed[0]).astype(BF16).astype(F32),
                jnp.where(swap, mixed[0], mixed[1]).astype(BF16).astype(F32),
            )
            for half in range(2):
                r0 = half * SPAN + tile * TOKENS
                rows = slice(r0, r0 + TOKENS)
                for a in range(GROUP):
                    cols = slice(HEAD_DIM * a, HEAD_DIM * (a + 1))
                    part = halves[half][TOKENS * a : TOKENS * (a + 1)]
                    to_ref[rows, cols] = (h_ref[rows, cols].astype(F32) + part).astype(BF16)

    def relay_wave(layer, g_ref, dx):
        @pl.when(dx > 0)
        def _():
            relay(layer, g_ref, dx * SIDE)

        for dy in range(1, SIDE):
            relay(layer, g_ref, dx * SIDE + dy)

    def relayed_wave(layer, g_ref, dx):
        @pl.when(dx == 0)
        def _():
            relayed(layer, g_ref, 0, True)

        @pl.when(dx > 0)
        def _():
            relayed(layer, g_ref, dx * SIDE)

        for dy in range(1, SIDE):
            relayed(layer, g_ref, dx * SIDE + dy)

    finish_sums(0, sq0)

    @pl.when(section == 1)
    def _():
        remote(gain_own, gain0, gain_sem.at[0], gain_sem.at[1], s=0).wait_recv()
        for d in range(1, HEADS_AXIS):
            got = head_at(d, -1)
            remote(
                zsend.at[got], zrecv1.at[got], zs_sem.at[d], zr1_sem.at[d], h=got
            ).wait_recv()

    every = range(TILES)
    make_queries(x_ref, sq0, gain0, every)

    def early(dx, carry):
        @pl.when(dx < SIDE - 2)
        def _():
            relay_wave(0, g0_ref, dx + 2)

        @pl.when((section == 1) & (dx == SECOND_AFTER))
        def _():
            begin_layer(1, zrecv1, g1_ref)

        relayed_wave(0, g0_ref, dx)
        attend_wave(g0_ref, dx, every)
        return carry

    relay_wave(0, g0_ref, jnp.int32(0))
    relay_wave(0, g0_ref, jnp.int32(1))
    lax.fori_loop(0, SIDE - 1, early, 0)

    first, rest = range(0, 1), range(1, TILES)

    def squares_of(part, sq):
        sq_own[part] = square_rows(
            [y_ref[:, HEAD_DIM * a : HEAD_DIM * (a + 1)].astype(F32) for a in range(GROUP)]
        )
        sq[head] = sq_own[part]
        send_sums(part, sq)

    y_ref[...] = x_ref[...]
    relayed_wave(0, g0_ref, jnp.int32(SIDE - 1))
    attend_wave(g0_ref, SIDE - 1, first)
    write_rows(x_ref, y_ref, first)

    @pl.when(section == 1)
    def _():
        squares_of(1, sq1.at[0])

    attend_wave(g0_ref, SIDE - 1, rest)
    write_rows(x_ref, y_ref, rest)

    @pl.when(section == 0)
    def _():
        out_ref[...] = y_ref[...]

    @pl.when(section == 1)
    def _():
        squares_of(2, sq1.at[1])
        clear_state()
        relay_wave(1, g1_ref, jnp.int32(0))
        sent(0, g0_ref)
        for d in range(1, HEADS_AXIS):
            peer = head_at(d, 1)
            remote(
                zsend.at[peer], zrecv1.at[head], zs_sem.at[d], zr1_sem.at[d], h=peer
            ).wait_send()
        relay_wave(1, g1_ref, jnp.int32(1))
        finish_sums(1, sq1.at[0])
        make_queries(y_ref, sq1.at[0], gain_own, first)

        def with_relay(dx, carry):
            @pl.when(dx < SIDE - 2)
            def _():
                relay_wave(1, g1_ref, dx + 2)

            relayed_wave(1, g1_ref, dx)
            attend_wave(g1_ref, dx, first)
            return carry

        lax.fori_loop(0, SIDE, with_relay, 0)
        write_rows(y_ref, out_ref, first)
        sent(1, g1_ref)
        finish_sums(2, sq1.at[1])
        make_queries(y_ref, sq1.at[1], gain_own, rest)

        def without_relay(dx, carry):
            attend_wave(g1_ref, dx, rest)
            return carry

        lax.fori_loop(0, SIDE, without_relay, 0)
        write_rows(y_ref, out_ref, rest)

    @pl.when(section == 0)
    def _():
        sent(0, g0_ref)
        for d in range(HEADS_AXIS):
            peer = head_at(d, 1)
            remote(
                zsend.at[peer], zrecv0.at[head], zs_sem.at[d], zr0_sem.at[d], s=1, h=peer
            ).wait_send()
            if d > 0:
                remote(
                    zsend.at[peer],
                    zrecv0.at[head],
                    zs_sem.at[HEADS_AXIS + d],
                    zr0_sem.at[d],
                    h=peer,
                ).wait_send()
        remote(gain_own, gain0, gain_sem.at[0], gain_sem.at[1], s=1).wait_send()


def local(residual_incoming, norm_gain, key_states, value_states, positions):
    vmem = pl.BlockSpec(memory_space=pltpu.VMEM)
    smem = pl.BlockSpec(memory_space=pltpu.SMEM)
    dma = pltpu.SemaphoreType.DMA
    state = pltpu.VMEM((2, TILES, TILE, HEAD_DIM), F32)
    pieces = pltpu.VMEM((HEADS_AXIS, 32, HEAD_DIM), BF16)
    blocks = pltpu.VMEM((CTX, SLOT, HEAD_DIM), BF16)
    anywhere = pl.BlockSpec(memory_space=pltpu.HBM)
    rows = pltpu.VMEM((ROWS, HEAD_DIM), BF16)
    out = pl.pallas_call(
        sublayers_kernel,
        name="sublayers",
        out_shape=jax.ShapeDtypeStruct(residual_incoming.shape, BF16),
        in_specs=[anywhere, anywhere, smem, anywhere, anywhere],
        out_specs=vmem,
        scratch_shapes=[
            pltpu.VMEM(residual_incoming.shape, BF16),
            rows,
            rows,
            pieces,
            pieces,
            pieces,
            pltpu.VMEM((2, SLOT, HEAD_DIM), BF16),
            blocks,
            blocks,
            pltpu.VMEM((GROUP, HEAD_DIM), F32),
            pltpu.VMEM((GROUP, HEAD_DIM), F32),
            pltpu.VMEM((3, 8, HEAD_DIM), F32),
            pltpu.VMEM((HEADS_AXIS, 8, HEAD_DIM), F32),
            pltpu.VMEM((2, HEADS_AXIS, 8, HEAD_DIM), F32),
            pltpu.VMEM(residual_incoming.shape, BF16),
            pltpu.VMEM((2, TILES, TILE, HEAD_DIM), BF16),
            state,
            state,
            state,
            pltpu.VMEM((TILES, TILE, HEAD_DIM), jnp.int32),
            dma((2 * HEADS_AXIS,)),
            dma((HEADS_AXIS,)),
            dma((HEADS_AXIS,)),
            dma((3, HEADS_AXIS)),
            dma((3, HEADS_AXIS)),
            dma((2,)),
            dma((2, CHIPS)),
            dma((2, CHIPS)),
            dma((2, CHIPS)),
            dma((2, CHIPS)),
            dma((4,)),
        ],
        compiler_params=pltpu.CompilerParams(
            collective_id=0, has_side_effects=True, vmem_limit_bytes=62 * 2**20
        ),
    )(
        key_states.reshape(ROWS, HEAD_DIM),
        value_states.reshape(ROWS, HEAD_DIM),
        positions,
        residual_incoming,
        norm_gain.reshape(-1, HEAD_DIM),
    )
    return out[None]


def solution(mesh):
    placed = (
        P("ctx", "head"),
        P("section", None),
        P("section", ("ctx", "head"), None, None),
        P("section", ("ctx", "head"), None, None),
        P(("ctx", "head")),
    )
    return jax.shard_map(
        local, mesh=mesh, in_specs=placed, out_specs=P("section", "ctx", "head"), check_vma=False
    )
```

```python
import math

import jax
import jax.numpy as jnp
from jax import lax
from jax.experimental import pallas as pl
from jax.experimental.pallas import tpu as pltpu
from jax.sharding import PartitionSpec as P

HEAD_DIM = 128
SPAN = 48
EPSILON = 1e-05
ROWS = 2 * SPAN
SLOT = 2 * ROWS + 16
CHIPS = 16
SIDE = 4
HEADS_AXIS = 8
SECTIONS = 2
CTX = 2 * CHIPS
RUNS = 2 * CTX
PIECE = ROWS // HEADS_AXIS
WAVE = 2 * SIDE
TOKENS = 16
TILE = 16 * TOKENS
TILES = SPAN // TOKENS
GROUP = 16
SCALE = math.log2(math.e) / math.sqrt(HEAD_DIM)
SECOND_AFTER = 1
ORDER = tuple(SIDE * dx + dy for dx in range(SIDE) for dy in (1, 3, 2, 0) if dx + dy > 0)
F32 = jnp.float32
BF16 = jnp.bfloat16


def iota(shape, dim):
    return lax.broadcasted_iota(jnp.int32, shape, dim)


def first_run_of(pos_ref, head):
    run = pos_ref[0] // SPAN
    return jnp.where(head * PIECE < SPAN, run, RUNS - 1 - run)


def square_rows(wide_tiles):
    total = wide_tiles[0] * wide_tiles[0]
    for tile in wide_tiles[1:]:
        total = total + tile * tile
    padded = jnp.concatenate([total, jnp.zeros((HEAD_DIM - ROWS, HEAD_DIM), F32)], axis=0)
    turned = padded.T
    part = turned[0:8]
    for k in range(1, HEAD_DIM // 8):
        part = part + turned[8 * k : 8 * k + 8]
    return part


def column_scale(parts):
    total = parts[0]
    for d in range(1, HEADS_AXIS):
        total = total + parts[d]
    total = jnp.sum(total, axis=0, keepdims=True)
    scale = lax.rsqrt(total * (1.0 / (HEADS_AXIS * GROUP * HEAD_DIM)) + EPSILON)
    return jnp.broadcast_to(scale, (HEAD_DIM, HEAD_DIM)).T


def update(q, k, v, old, gap, place):
    s = lax.dot_general(q, k, (((1,), (1,)), ((), ())), preferred_element_type=F32)
    parts = s.shape[1] // HEAD_DIM
    s = jnp.where(gap <= jnp.concatenate([place] * parts, axis=1), s, -1e30)
    new = jnp.maximum(old[0], jnp.max(s, axis=1, keepdims=True))
    p = jnp.exp2((s - jnp.concatenate([new] * parts, axis=1)) * SCALE)
    both = jnp.dot(p.astype(BF16), v, preferred_element_type=F32)
    factor = jnp.exp2((old[0] - new) * SCALE)
    return new, old[1] * factor + both[:, HEAD_DIM:], old[2] * factor + both[:, :HEAD_DIM]


def sublayers_kernel(
    k_ref,
    v_ref,
    pos_ref,
    x_hbm,
    gain_ref,
    out_ref,
    x_ref,
    k_own,
    v_own,
    zsend,
    zrecv0,
    zrecv1,
    stage,
    g0_ref,
    g1_ref,
    gain0,
    gain_own,
    sq_own,
    sq0,
    sq1,
    y_ref,
    q_ref,
    m_ref,
    l_ref,
    acc_ref,
    place_ref,
    zs_sem,
    zr0_sem,
    zr1_sem,
    sqs_sem,
    sqr_sem,
    gain_sem,
    gs_sem,
    gr_sem,
    fs_sem,
    fr_sem,
    in_sem,
):
    section = lax.axis_index("section")
    ctx = lax.axis_index("ctx")
    head = lax.axis_index("head")
    chip = ctx // 2
    core = ctx % 2
    cx = chip // SIDE
    cy = chip % SIDE
    sibling = ctx + 1 - 2 * core

    def at(offset, sign):
        dx, dy = offset // SIDE, offset % SIDE
        px = lax.rem(cx + sign * dx + SIDE, SIDE)
        py = lax.rem(cy + sign * dy + SIDE, SIDE)
        return (px * SIDE + py) * 2 + core

    def head_at(offset, sign):
        return lax.rem(head + sign * offset + HEADS_AXIS, HEADS_AXIS)

    def remote(src, dst, send, recv, s=None, c=None, h=None):
        target = (
            section if s is None else s,
            ctx if c is None else c,
            head if h is None else h,
        )
        return pltpu.make_async_remote_copy(
            src_ref=src,
            dst_ref=dst,
            send_sem=send,
            recv_sem=recv,
            device_id=target,
            device_id_type=pl.DeviceIdType.MESH,
        )

    own_rows = pl.ds(pl.multiple_of(head * GROUP, GROUP), GROUP)
    fetches = [
        pltpu.make_async_copy(src, dst, in_sem.at[i])
        for i, (src, dst) in enumerate(
            (
                (k_ref, k_own),
                (v_ref, v_own),
                (x_hbm, x_ref),
                (gain_ref.at[own_rows], gain_own),
            )
        )
    ]
    for fetch in fetches:
        fetch.start()

    barrier = pltpu.get_barrier_semaphore()

    def greet(s, c, h):
        pl.semaphore_signal(
            barrier, inc=1, device_id=(s, c, h), device_id_type=pl.DeviceIdType.MESH
        )

    @pl.when(section == 1)
    def _():
        for d in range(HEADS_AXIS):
            greet(0, ctx, head_at(d, 1))

    for d in range(1, HEADS_AXIS):
        greet(section, ctx, head_at(d, 1))
    for d in range(1, CHIPS):
        greet(section, at(d, 1), head)
    greet(section, sibling, head)

    out_row = iota((HEAD_DIM, ROWS), 0)
    in_row = iota((HEAD_DIM, ROWS), 1)
    pick = (out_row % 16) * HEADS_AXIS + out_row // 16
    spread = jnp.where((in_row == pick) & (out_row % 16 < PIECE), 1.0, 0.0).astype(BF16)
    fetches[0].wait()
    fetches[1].wait()
    keys = jnp.dot(spread, k_own[...], preferred_element_type=F32).astype(BF16)
    values = jnp.dot(spread, v_own[...], preferred_element_type=F32).astype(BF16)
    for h in range(HEADS_AXIS):
        zsend[h, 0:16] = keys[16 * h : 16 * h + 16]
        zsend[h, 16:32] = values[16 * h : 16 * h + 16]
    first_run = first_run_of(pos_ref, head)
    swap = first_run >= CTX
    low = jnp.where(swap, RUNS - 1 - first_run, first_run)

    @pl.when(section == 0)
    def _():
        pl.semaphore_wait(barrier, 2 * HEADS_AXIS - 1 + CHIPS)
        for d in range(HEADS_AXIS):
            peer = head_at(d, 1)
            remote(
                zsend.at[peer],
                zrecv0.at[head],
                zs_sem.at[d],
                zr0_sem.at[d],
                s=1,
                h=peer,
            ).start()
            if d > 0:
                remote(
                    zsend.at[peer],
                    zrecv0.at[head],
                    zs_sem.at[HEADS_AXIS + d],
                    zr0_sem.at[d],
                    h=peer,
                ).start()
        zrecv0[head] = zsend[head]

    @pl.when(section == 1)
    def _():
        pl.semaphore_wait(barrier, HEADS_AXIS - 1 + CHIPS)
        for d in range(1, HEADS_AXIS):
            peer = head_at(d, 1)
            remote(
                zsend.at[peer],
                zrecv1.at[head],
                zs_sem.at[d],
                zr1_sem.at[d],
                h=peer,
            ).start()
        zrecv1[head] = zsend[head]

    def send_sums(part, sq):
        for d in range(1, HEADS_AXIS):
            remote(
                sq_own.at[part],
                sq.at[head],
                sqs_sem.at[part, d],
                sqr_sem.at[part, d],
                h=head_at(d, 1),
            ).start()

    def finish_sums(part, sq):
        for d in range(1, HEADS_AXIS):
            remote(
                sq_own.at[part],
                sq.at[head_at(d, -1)],
                sqs_sem.at[part, d],
                sqr_sem.at[part, d],
                h=head_at(d, 1),
            ).wait()

    fetches[2].wait()
    fetches[3].wait()
    sq_own[0] = square_rows(
        [x_ref[:, HEAD_DIM * a : HEAD_DIM * (a + 1)].astype(F32) for a in range(GROUP)]
    )
    sq0[head] = sq_own[0]
    send_sums(0, sq0)

    @pl.when(section == 0)
    def _():
        remote(gain_own, gain0, gain_sem.at[0], gain_sem.at[1], s=1).start()
        gain0[...] = gain_own[...]

    row = iota((2 * ROWS, 16 * 16), 0)
    col = iota((2 * ROWS, 16 * 16), 1)
    turn = jnp.where(swap, SPAN, 0)
    place = lax.rem(row + turn, ROWS)
    source = (place // PIECE) * 32 + place % PIECE + jnp.where(row >= ROWS, 16, 0)
    compact = jnp.where(col == source, 1.0, 0.0).astype(BF16)
    meta = (jnp.zeros((16, HEAD_DIM), F32) + low.astype(F32)).astype(BF16)

    def begin_layer(layer, zrecv, g_ref):
        pieces = zrecv[...].reshape(16 * 16, HEAD_DIM)
        block = jnp.dot(compact, pieces, preferred_element_type=F32).astype(BF16)
        stage[layer, 0 : 2 * ROWS] = block
        stage[layer, 2 * ROWS : SLOT] = meta
        remote(
            stage.at[layer],
            g_ref.at[ctx],
            fs_sem.at[layer, 0],
            fr_sem.at[layer, 0],
            c=sibling,
        ).start()
        for d in ORDER:
            remote(
                stage.at[layer],
                g_ref.at[ctx],
                gs_sem.at[layer, d],
                gr_sem.at[layer, d],
                c=at(d, 1),
            ).start()
        g_ref[ctx, 0 : 2 * ROWS] = block
        g_ref[ctx, 2 * ROWS : SLOT] = meta

    def relay(layer, g_ref, d):
        got = at(d, -1)
        remote(
            stage.at[layer],
            g_ref.at[got],
            gs_sem.at[layer, d],
            gr_sem.at[layer, d],
            c=at(d, 1),
        ).wait_recv()
        remote(
            g_ref.at[got],
            g_ref.at[got],
            fs_sem.at[layer, d],
            fr_sem.at[layer, d],
            c=sibling,
        ).start()

    def relayed(layer, g_ref, d, own=False):
        slot = at(d, -1) + 1 - 2 * core
        mine = stage.at[layer] if own else g_ref.at[at(d, -1)]
        remote(
            mine, g_ref.at[slot], fs_sem.at[layer, d], fr_sem.at[layer, d], c=sibling
        ).wait_recv()

    def sent(layer, g_ref):
        for d in range(CHIPS):
            if d > 0:
                remote(
                    stage.at[layer],
                    g_ref.at[ctx],
                    gs_sem.at[layer, d],
                    gr_sem.at[layer, d],
                    c=at(d, 1),
                ).wait_send()
            mine = stage.at[layer] if d == 0 else g_ref.at[at(d, -1)]
            remote(
                mine, g_ref.at[ctx], fs_sem.at[layer, d], fr_sem.at[layer, d], c=sibling
            ).wait_send()

    @pl.when(section == 1)
    def _():
        remote(
            zsend.at[head], zrecv0.at[head], zs_sem.at[0], zr0_sem.at[0], s=0
        ).wait_recv()

    for d in range(1, HEADS_AXIS):
        got = head_at(d, -1)
        remote(
            zsend.at[got], zrecv0.at[got], zs_sem.at[d], zr0_sem.at[d], h=got
        ).wait_recv()
    begin_layer(0, zrecv0, g0_ref)

    def clear_state():
        m_ref[...] = jnp.full(m_ref.shape, -1e30, F32)
        l_ref[...] = jnp.zeros(l_ref.shape, F32)
        acc_ref[...] = jnp.zeros(acc_ref.shape, F32)

    clear_state()
    place_shape = (TILES, TILE, HEAD_DIM)
    place_ref[...] = iota(place_shape, 0) * TOKENS + iota(place_shape, 1) % TOKENS

    def make_queries(h_ref, sq, gain, tiles):
        column = column_scale([sq[d] for d in range(HEADS_AXIS)])
        for tile in tiles:
            for a in range(GROUP):
                cols = slice(HEAD_DIM * a, HEAD_DIM * (a + 1))
                qs = []
                for half in range(2):
                    rows = slice(half * SPAN + tile * TOKENS, half * SPAN + (tile + 1) * TOKENS)
                    wide = h_ref[rows, cols].astype(F32)
                    qs.append(wide * column[rows] * gain[a : a + 1, :])
                to = slice(TOKENS * a, TOKENS * (a + 1))
                q_ref[0, tile, to, :] = jnp.where(swap, qs[1], qs[0]).astype(BF16)
                q_ref[1, tile, to, :] = jnp.where(swap, qs[0], qs[1]).astype(BF16)

    def flat(ref, kind, tiles):
        rows = ref[kind, tiles.start : tiles.stop]
        return rows.reshape(len(tiles) * TILE, HEAD_DIM)

    def update_rows(kind, tiles, k, v, gap):
        old = tuple(flat(ref, kind, tiles) for ref in (m_ref, l_ref, acc_ref))
        place = place_ref[tiles.start : tiles.stop].reshape(len(tiles) * TILE, HEAD_DIM)
        state = update(flat(q_ref, kind, tiles), k, v, old, gap, place)
        for ref, part in zip((m_ref, l_ref, acc_ref), state):
            ref[kind, tiles.start : tiles.stop] = part.reshape(len(tiles), TILE, HEAD_DIM)

    def attend_wave(g_ref, dx, tiles):
        row_of = lax.rem(cx - dx + SIDE, SIDE)
        here = pl.ds(row_of * WAVE, WAVE)
        size = 2 * WAVE * SPAN
        lane = iota((1, size), 1)
        tag = jnp.zeros((1, size), F32)
        tags = g_ref[here, 2 * ROWS : SLOT, :].astype(F32)
        for i in range(WAVE):
            wide = jnp.concatenate([tags[i, 0:1, :]] * (size // HEAD_DIM), axis=1)
            tag = jnp.where(lane // ROWS == i, wide, tag)
        at_row = lane % ROWS
        run = tag.astype(jnp.int32)
        run = jnp.where(at_row >= SPAN, RUNS - 1 - run, run)
        key_pos = run * SPAN + at_row % SPAN
        low_lane = iota((1, size // 2), 1)
        tag = jnp.zeros((1, size // 2), F32)
        for i in range(WAVE):
            wide = jnp.concatenate([tags[i, 0:1, :]] * (size // 2 // HEAD_DIM), axis=1)
            tag = jnp.where(low_lane // SPAN == i, wide, tag)
        low_pos = tag.astype(jnp.int32) * SPAN + low_lane % SPAN
        k = g_ref[here, 0:ROWS, :].reshape(size, HEAD_DIM)
        v = g_ref[here, ROWS : 2 * ROWS, :].reshape(size, HEAD_DIM)
        k_low = g_ref[here, 0:SPAN, :].reshape(size // 2, HEAD_DIM)
        v_low = g_ref[here, ROWS : ROWS + SPAN, :].reshape(size // 2, HEAD_DIM)
        ones = jnp.ones((size, HEAD_DIM), BF16)
        v = jnp.concatenate([v, ones], axis=1)
        v_low = jnp.concatenate([v_low, ones[: size // 2]], axis=1)
        update_rows(1, tiles, k, v, key_pos - (RUNS - 1 - low) * SPAN)
        update_rows(0, tiles, k_low, v_low, low_pos - low * SPAN)

    def write_rows(h_ref, to_ref, tiles):
        for tile in tiles:
            mixed = []
            for kind in range(2):
                mixed.append(acc_ref[kind, tile] / l_ref[kind, tile])
            halves = (
                jnp.where(swap, mixed[1], mixed[0]).astype(BF16).astype(F32),
                jnp.where(swap, mixed[0], mixed[1]).astype(BF16).astype(F32),
            )
            for half in range(2):
                r0 = half * SPAN + tile * TOKENS
                rows = slice(r0, r0 + TOKENS)
                for a in range(GROUP):
                    cols = slice(HEAD_DIM * a, HEAD_DIM * (a + 1))
                    part = halves[half][TOKENS * a : TOKENS * (a + 1)]
                    to_ref[rows, cols] = (h_ref[rows, cols].astype(F32) + part).astype(BF16)

    def relay_wave(layer, g_ref, dx):
        @pl.when(dx > 0)
        def _():
            relay(layer, g_ref, dx * SIDE)

        for dy in range(1, SIDE):
            relay(layer, g_ref, dx * SIDE + dy)

    def relayed_wave(layer, g_ref, dx):
        @pl.when(dx == 0)
        def _():
            relayed(layer, g_ref, 0, True)

        @pl.when(dx > 0)
        def _():
            relayed(layer, g_ref, dx * SIDE)

        for dy in range(1, SIDE):
            relayed(layer, g_ref, dx * SIDE + dy)

    finish_sums(0, sq0)

    @pl.when(section == 1)
    def _():
        remote(gain_own, gain0, gain_sem.at[0], gain_sem.at[1], s=0).wait_recv()
        for d in range(1, HEADS_AXIS):
            got = head_at(d, -1)
            remote(
                zsend.at[got], zrecv1.at[got], zs_sem.at[d], zr1_sem.at[d], h=got
            ).wait_recv()

    every = range(TILES)
    make_queries(x_ref, sq0, gain0, every)

    def early(dx, carry):
        relay_wave(0, g0_ref, dx + 1)

        @pl.when((section == 1) & (dx == SECOND_AFTER))
        def _():
            begin_layer(1, zrecv1, g1_ref)

        relayed_wave(0, g0_ref, dx)
        attend_wave(g0_ref, dx, every)
        return carry

    relay_wave(0, g0_ref, jnp.int32(0))
    lax.fori_loop(0, SIDE - 1, early, 0)

    first, rest = range(0, 1), range(1, TILES)

    def squares_of(part, sq):
        sq_own[part] = square_rows(
            [y_ref[:, HEAD_DIM * a : HEAD_DIM * (a + 1)].astype(F32) for a in range(GROUP)]
        )
        sq[head] = sq_own[part]
        send_sums(part, sq)

    y_ref[...] = x_ref[...]
    relayed_wave(0, g0_ref, jnp.int32(SIDE - 1))
    attend_wave(g0_ref, SIDE - 1, first)
    write_rows(x_ref, y_ref, first)

    @pl.when(section == 1)
    def _():
        squares_of(1, sq1.at[0])

    attend_wave(g0_ref, SIDE - 1, rest)
    write_rows(x_ref, y_ref, rest)

    @pl.when(section == 0)
    def _():
        out_ref[...] = y_ref[...]

    @pl.when(section == 1)
    def _():
        squares_of(2, sq1.at[1])
        clear_state()
        relay_wave(1, g1_ref, jnp.int32(0))
        sent(0, g0_ref)
        for d in range(1, HEADS_AXIS):
            peer = head_at(d, 1)
            remote(
                zsend.at[peer], zrecv1.at[head], zs_sem.at[d], zr1_sem.at[d], h=peer
            ).wait_send()
        finish_sums(1, sq1.at[0])
        make_queries(y_ref, sq1.at[0], gain_own, first)

        def with_relay(dx, carry):
            @pl.when(dx < SIDE - 1)
            def _():
                relay_wave(1, g1_ref, dx + 1)

            relayed_wave(1, g1_ref, dx)
            attend_wave(g1_ref, dx, first)
            return carry

        lax.fori_loop(0, SIDE, with_relay, 0)
        write_rows(y_ref, out_ref, first)
        sent(1, g1_ref)
        finish_sums(2, sq1.at[1])
        make_queries(y_ref, sq1.at[1], gain_own, rest)

        def without_relay(dx, carry):
            attend_wave(g1_ref, dx, rest)
            return carry

        lax.fori_loop(0, SIDE, without_relay, 0)
        write_rows(y_ref, out_ref, rest)

    @pl.when(section == 0)
    def _():
        sent(0, g0_ref)
        for d in range(HEADS_AXIS):
            peer = head_at(d, 1)
            remote(
                zsend.at[peer], zrecv0.at[head], zs_sem.at[d], zr0_sem.at[d], s=1, h=peer
            ).wait_send()
            if d > 0:
                remote(
                    zsend.at[peer],
                    zrecv0.at[head],
                    zs_sem.at[HEADS_AXIS + d],
                    zr0_sem.at[d],
                    h=peer,
                ).wait_send()
        remote(gain_own, gain0, gain_sem.at[0], gain_sem.at[1], s=1).wait_send()


def local(residual_incoming, norm_gain, key_states, value_states, positions):
    vmem = pl.BlockSpec(memory_space=pltpu.VMEM)
    smem = pl.BlockSpec(memory_space=pltpu.SMEM)
    dma = pltpu.SemaphoreType.DMA
    state = pltpu.VMEM((2, TILES, TILE, HEAD_DIM), F32)
    pieces = pltpu.VMEM((HEADS_AXIS, 32, HEAD_DIM), BF16)
    blocks = pltpu.VMEM((CTX, SLOT, HEAD_DIM), BF16)
    anywhere = pl.BlockSpec(memory_space=pltpu.HBM)
    rows = pltpu.VMEM((ROWS, HEAD_DIM), BF16)
    out = pl.pallas_call(
        sublayers_kernel,
        name="sublayers",
        out_shape=jax.ShapeDtypeStruct(residual_incoming.shape, BF16),
        in_specs=[anywhere, anywhere, smem, anywhere, anywhere],
        out_specs=vmem,
        scratch_shapes=[
            pltpu.VMEM(residual_incoming.shape, BF16),
            rows,
            rows,
            pieces,
            pieces,
            pieces,
            pltpu.VMEM((2, SLOT, HEAD_DIM), BF16),
            blocks,
            blocks,
            pltpu.VMEM((GROUP, HEAD_DIM), F32),
            pltpu.VMEM((GROUP, HEAD_DIM), F32),
            pltpu.VMEM((3, 8, HEAD_DIM), F32),
            pltpu.VMEM((HEADS_AXIS, 8, HEAD_DIM), F32),
            pltpu.VMEM((2, HEADS_AXIS, 8, HEAD_DIM), F32),
            pltpu.VMEM(residual_incoming.shape, BF16),
            pltpu.VMEM((2, TILES, TILE, HEAD_DIM), BF16),
            state,
            state,
            state,
            pltpu.VMEM((TILES, TILE, HEAD_DIM), jnp.int32),
            dma((2 * HEADS_AXIS,)),
            dma((HEADS_AXIS,)),
            dma((HEADS_AXIS,)),
            dma((3, HEADS_AXIS)),
            dma((3, HEADS_AXIS)),
            dma((2,)),
            dma((2, CHIPS)),
            dma((2, CHIPS)),
            dma((2, CHIPS)),
            dma((2, CHIPS)),
            dma((4,)),
        ],
        compiler_params=pltpu.CompilerParams(
            collective_id=0, has_side_effects=True, vmem_limit_bytes=62 * 2**20
        ),
    )(
        key_states.reshape(ROWS, HEAD_DIM),
        value_states.reshape(ROWS, HEAD_DIM),
        positions,
        residual_incoming,
        norm_gain.reshape(-1, HEAD_DIM),
    )
    return out[None]


def solution(mesh):
    placed = (
        P("ctx", "head"),
        P("section", None),
        P("section", ("ctx", "head"), None, None),
        P("section", ("ctx", "head"), None, None),
        P(("ctx", "head")),
    )
    return jax.shard_map(
        local, mesh=mesh, in_specs=placed, out_specs=P("section", "ctx", "head"), check_vma=False
    )
```
